128 devices in a mesh: pop: 16 (over y_lo, x, core), tp: 8 (over z, y_hi).
Axes of the slice: x: 4, y: 4 (y_hi: 2, y_lo: 2; y = y_hi * 2 + y_lo), z: 4, core: 2. Of those that a mesh axis runs over, the one named last changes fastest.
Arguments:
- hidden_units: bfloat16 [16, 128, 18944], P('pop', None, 'tp'), may hold values from -6 to 6
- residual: bfloat16 [16, 128, 3584], P('pop'), may hold values from -6 to 6
- down_weight: bfloat16 [18944, 3584], P('tp'), may hold values from -0.046875 to 0.046875
- norm_gain: float32 [3584], replicated, may hold values from 0.5 to 1.5
- head: bfloat16 [3584, 98304], P(None, ('pop', 'tp')), may hold values from -16 to 16
- labels: int32 [16, 128], P('pop'), may hold values from 0 to 98303
- answer_start: int32 [16], replicated, may hold values from 32 to 96
- seeds: int32 [16], replicated, may hold values from 0 to 1073741823
- signs: int32 [32], replicated, may hold values from -1 to 1, as said below
Outputs:
- fitness: float32 [32], replicated
- update_direction: float32 [18944, 3584], P(('pop', 'tp'))
The draws below stay inside these ranges and needn't reach their ends.
Inputs may be any that keep to these rules, and one draw needn't show every extreme that they name: Members 2 p and 2 p + 1 carry opposite signs.
All inputs are finite; a program needn't handle non-finite values.
Results may differ from the reference program's by a relative error of at most 0.007.
The reference program's roundings to bfloat16 on the way count: a program that leaves them out, or rounds other values in their place, can miss the bound.
Values may be sent and summed in bfloat16 or wider, within the bound.
No kernel may reach another device: no remote copies, remote signals or barrier semaphores. Data moves between devices by JAX's collectives and lax.ppermute only.
A program may use at most 192 MiB of HBM per device.

```python
import math
import jax
import jax.numpy as jnp
import numpy as np
from jax import lax

D = 3584
FF = 18944
V = 98304
TOK = 128
PAIRS = 16
MEMBERS = 32


def draw_head(key, part):
    key = jax.random.fold_in(key, 11)
    entry_key = jax.random.fold_in(key, 0)
    weights = jax.random.normal(entry_key, (D, V), jnp.float32) * (3.0 * D ** (-0.5))
    return jnp.clip(weights, -16.0, 16.0).astype(jnp.bfloat16)


def draw_answer_start(key, part):
    key = jax.random.fold_in(key, 23)
    value_key, order_key = jax.random.split(key)
    lowest = TOK // 4
    highest = 3 * TOK // 4
    starts = jax.random.randint(value_key, (PAIRS,), lowest, highest + 1)
    order = jax.random.permutation(order_key, PAIRS)
    starts = starts.at[order[0]].set(lowest).at[order[1]].set(highest)
    return starts.astype(jnp.int32)


def draw_signs(key, part):
    key = jax.random.fold_in(key, 37)
    leading = jax.random.randint(key, (PAIRS,), 0, 2) * 2 - 1
    return jnp.stack([leading, -leading], axis=1).reshape(MEMBERS).astype(jnp.int32)


def touch_ends(values, rng, smallest, largest):
    shape = values.shape
    index_at = [jax.random.randint(jax.random.fold_in(rng, axis), (), 0, shape[axis]) for axis in range(len(shape))]
    values = values.at[tuple(index_at)].set(smallest)
    longest = shape.index(max(shape))
    index_at[longest] = (index_at[longest] + 1) % shape[longest]
    return values.at[tuple(index_at)].set(largest)


def levels(key, shape, cuts, least, top_value):
    loudness, own = 1.0, jax.random.fold_in(key, 6)
    for position, blocks in cuts:
        draws = jnp.exp(jax.random.uniform(jax.random.fold_in(own, position), (blocks,), jnp.float32, least / len(cuts), top_value / len(cuts)))
        loudness = loudness * jnp.repeat(draws, shape[position] // blocks).reshape([-1 if axis == position else 1 for axis in range(len(shape))])
    return loudness


def wide_ids(own_key, extent, number_of, slope):
    loads = [min(1 << octave, number_of + 1 - (1 << octave)) * (1 << 20) // math.isqrt((1 << octave) ** slope) + 1 for octave in range((number_of + 1).bit_length()) if 1 << octave <= number_of]
    width = 1 + sum(loads) // (1 << 30)
    grid = np.cumsum(np.array([max(1, weight // width) for weight in loads]))
    pick = jax.random.randint(jax.random.fold_in(own_key, 1), extent, 0, int(grid[len(loads) - 1]))
    start = jnp.left_shift(1, jnp.searchsorted(jnp.asarray(grid, jnp.int32), pick, side="right").astype(jnp.int32))
    standing = start - 1 + jax.random.randint(jax.random.fold_in(own_key, 4), extent, 0, 1 << 30) % jnp.minimum(start, number_of + 1 - start)
    return jax.random.permutation(jax.random.fold_in(own_key, 2), number_of)[standing].astype(jnp.int32)


def scatter_about(key, shape, spread, reach, cuts=(), kind=jnp.bfloat16):
    values = spread * jax.random.normal(key, shape, jnp.float32)
    if cuts:
        values = values * levels(key, shape, cuts, -0.22, 0.18)
    return jnp.clip(values, -reach, reach).astype(kind)


def setup_inputs(seed: int = 0) -> dict:
    key_list = jax.random.split(jax.random.key(seed), 10)
    hidden_units = scatter_about(key_list[0], (PAIRS, TOK, FF), 1.0, 6.0, ((0, 16), (2, 8)))
    residual = scatter_about(key_list[1], (PAIRS, TOK, D), 1.0, 6.0, ((0, 16),))
    down_weight = scatter_about(key_list[2], (FF, D), FF ** -0.5, 0.046875, ((0, 8),))
    norm_gain = jnp.clip(1.0 + 0.1 * jax.random.normal(key_list[3], (D,), jnp.float32), 0.5, 1.5)
    head = draw_head(jax.random.fold_in(key_list[9], 71), 0)
    labels = touch_ends(wide_ids(key_list[5], (PAIRS, TOK), V, 2), jax.random.fold_in(key_list[5], 3), 0, V - 1).astype(jnp.int32)
    answer_start = draw_answer_start(jax.random.fold_in(key_list[9], 71), 0)
    seeds = touch_ends(jax.random.randint(key_list[7], (PAIRS,), 0, 1073741824), jax.random.fold_in(key_list[7], 1), 0, 1073741823).astype(jnp.int32)
    signs = draw_signs(jax.random.fold_in(key_list[9], 71), 0)
    return {"hidden_units": hidden_units, "residual": residual, "down_weight": down_weight, "norm_gain": norm_gain, "head": head, "labels": labels, "answer_start": answer_start, "seeds": seeds, "signs": signs}


root_three = 1.7320508075688772

def mix_bits(hashed):
    hashed = jnp.bitwise_xor(hashed, lax.shift_right_logical(hashed, jnp.full_like(hashed, 15)))
    hashed = hashed * jnp.int32(739982445)
    hashed = jnp.bitwise_xor(hashed, lax.shift_right_logical(hashed, jnp.full_like(hashed, 12)))
    hashed = hashed * jnp.int32(695872825)
    hashed = jnp.bitwise_xor(hashed, lax.shift_right_logical(hashed, jnp.full_like(hashed, 15)))
    return hashed

def noise_block(pair_seed, first_row, row_count, col_count):
    row_ids = (first_row + jnp.arange(row_count, dtype=jnp.int32))[:, None]
    col_ids = jnp.arange(col_count, dtype=jnp.int32)[None, :]
    hashed = row_ids * jnp.int32(col_count) + col_ids + pair_seed * jnp.int32(1540483477)
    hashed = mix_bits(jnp.bitwise_xor(mix_bits(hashed), jnp.int32(1013904223)))
    uniform_bits = jnp.bitwise_and(hashed, jnp.int32(16777215)).astype(jnp.float32)
    return (((uniform_bits + 0.5) * (2.0 / 16777216.0) - 1.0) * root_three).astype(jnp.bfloat16)

def reference(hidden_units, residual, down_weight, norm_gain, head, labels, answer_start, seeds, signs):
    noise_scale = 0.25 * FF ** (-0.5)
    positions = jnp.arange(TOK, dtype=jnp.int32)

    def pair_fitness(pair_index):
        noise_full = noise_block(seeds[pair_index], jnp.int32(0), FF, D)
        base_out = jnp.dot(hidden_units[pair_index], down_weight, preferred_element_type=jnp.float32)
        probe_out = jnp.dot(hidden_units[pair_index], noise_full, preferred_element_type=jnp.float32)
        pair_signs = lax.dynamic_slice_in_dim(signs, pair_index * 2, 2).astype(jnp.float32)
        layer_out = residual[pair_index].astype(jnp.float32)[None] + base_out[None] + pair_signs[:, None, None] * noise_scale * probe_out[None]
        mean_square = lax.optimization_barrier(jnp.mean(layer_out * layer_out, axis=2, keepdims=True))
        normed = (layer_out * lax.rsqrt(mean_square + 1e-06) * norm_gain).astype(jnp.bfloat16)
        logits = jnp.dot(normed.reshape(2 * TOK, D), head, preferred_element_type=jnp.float32)
        row_labels = jnp.concatenate([labels[pair_index], labels[pair_index]])
        target = jnp.take_along_axis(logits, row_labels[:, None], axis=1)[:, 0]
        log_prob = (target - jax.nn.logsumexp(logits, axis=1)).reshape(2, TOK)
        answer_mask = (positions >= answer_start[pair_index]).astype(jnp.float32)
        answer_count = (TOK - answer_start[pair_index]).astype(jnp.float32)
        return lax.optimization_barrier(jnp.sum(log_prob * answer_mask[None], axis=1)) / answer_count
    fitness = lax.map(pair_fitness, jnp.arange(PAIRS, dtype=jnp.int32)).reshape(MEMBERS)
    fitness_gap = lax.optimization_barrier(jnp.sum((fitness * signs.astype(jnp.float32)).reshape(PAIRS, 2), axis=1))

    def add_pair(pair_index, running):
        term = noise_block(seeds[pair_index], jnp.int32(0), FF, D).astype(jnp.float32)
        return running + fitness_gap[pair_index] * term
    update_direction = lax.fori_loop(0, PAIRS, add_pair, jnp.zeros((FF, D), jnp.float32))
    return (fitness, update_direction)
```

```python
import functools

import jax
import jax.numpy as jnp
from jax import lax
from jax.experimental import pallas as pl
from jax.experimental.pallas import tpu as pltpu
from jax.sharding import Mesh, PartitionSpec as P

FF = 18944
D = 3584
SKIP = 32
EXTRA = 128

MUL_A = 739982445
MUL_B = 695872825
SALT = 1013904223
SALT_MIXED = SALT ^ (SALT >> 15)
root_three = 1.7320508075688772

TP = ("z", "y_hi")
SAME_CORE = ("z", "y_hi", "y_lo", "x")


def shifted(hashed, places):
    return lax.shift_right_logical(hashed, jnp.full_like(hashed, places))


def noise_of(index):
    h = index ^ shifted(index, 15)
    h = h * jnp.int32(MUL_A)
    h = h ^ shifted(h, 12)
    h = h * jnp.int32(MUL_B)
    h = h ^ shifted(h, 30) ^ jnp.int32(SALT_MIXED)
    h = h * jnp.int32(MUL_A)
    h = h ^ shifted(h, 12)
    h = h * jnp.int32(MUL_B)
    bits = (h ^ shifted(h, 15)) & jnp.int32(16777215)
    return ((bits.astype(jnp.float32) - 8388607.5) * jnp.float32(root_three / 8388608.0)).astype(jnp.bfloat16)


def flat_index(rows, cols, width):
    return lax.broadcasted_iota(jnp.int32, (rows, cols), 0) * width + lax.broadcasted_iota(jnp.int32, (rows, cols), 1)


def probe_kernel(start_ref, hidden_ref, weight_ref, probe_ref, base_ref, *, first_col, tile):
    units = hidden_ref.shape[1]
    at = start_ref[0] + first_col + pl.program_id(0) * tile
    total = None
    for k in range(0, units, 256):
        depth = min(256, units - k)
        noise = noise_of(flat_index(depth, tile, D) + (at + k * D))
        part = jnp.dot(hidden_ref[SKIP:, k : k + depth], noise, preferred_element_type=jnp.float32)
        total = part if total is None else total + part
    probe_ref[...] = total.astype(probe_ref.dtype)
    if base_ref is not None:
        base_ref[...] = jnp.dot(
            hidden_ref[SKIP:, :], weight_ref[...], preferred_element_type=jnp.float32
        ).astype(base_ref.dtype)


def probe_call(start, hidden, weight, first_col, cols, tile, probe_type, base_type):
    tokens, units = hidden.shape
    steps = cols // tile
    rows = tokens - SKIP
    in_specs = [
        pl.BlockSpec(memory_space=pltpu.SMEM),
        pl.BlockSpec((tokens, units), lambda i: (0, 0)),
    ]
    out_specs = [pl.BlockSpec((rows, tile), lambda i: (0, i))]
    out_shape = [jax.ShapeDtypeStruct((rows, cols), probe_type)]
    kernel = functools.partial(probe_kernel, first_col=first_col, tile=tile)
    args = [start, hidden]
    if weight is not None:
        wide = D // steps
        in_specs.append(pl.BlockSpec((units, wide), lambda i: (0, i)))
        out_specs.append(pl.BlockSpec((rows, wide), lambda i: (0, i)))
        out_shape.append(jax.ShapeDtypeStruct((rows, D), base_type))
        args.append(weight)
    else:

        def kernel(start_ref, hidden_ref, probe_ref):
            probe_kernel(start_ref, hidden_ref, None, probe_ref, None, first_col=first_col, tile=tile)

    return pl.pallas_call(
        kernel,
        grid=(steps,),
        in_specs=in_specs,
        out_specs=out_specs,
        out_shape=out_shape,
        cost_estimate=pl.CostEstimate(
            flops=units * cols * 2000, bytes_accessed=units * cols, transcendentals=0
        ),
        compiler_params=pltpu.CompilerParams(vmem_limit_bytes=44 << 20),
        name="probe",
    )(*args)


def regenerate_kernel(start_ref, out_ref, *, width):
    at = start_ref[pl.program_id(0)]

    def rows16(r, _):
        first = pl.multiple_of(r * 16, 16)
        for c in range(0, D, width):
            out_ref[0, pl.ds(first, 16), c : c + width] = noise_of(flat_index(16, width, D) + (at + r * (16 * D) + c))
        return 0

    lax.fori_loop(0, out_ref.shape[1] // 16, rows16, 0)


def regenerate(starts, rows):
    pairs = starts.shape[0]
    padded = -(-rows // 16) * 16
    return pl.pallas_call(
        functools.partial(regenerate_kernel, width=512),
        grid=(pairs,),
        in_specs=[pl.BlockSpec(memory_space=pltpu.SMEM)],
        out_specs=pl.BlockSpec((1, padded, D), lambda p: (p, 0, 0)),
        out_shape=jax.ShapeDtypeStruct((pairs, padded, D), jnp.bfloat16),
        cost_estimate=pl.CostEstimate(
            flops=pairs * padded * D * 2000, bytes_accessed=pairs * padded * D * 2, transcendentals=0
        ),
        compiler_params=pltpu.CompilerParams(vmem_limit_bytes=44 << 20),
        name="regenerate",
    )(starts)


def logits_kernel(first_ref, rows_ref, own_ref, other_ref, out_ref, top_ref, sum_ref, hit_ref, *, steps_each):
    v = pl.program_id(1)
    tile = own_ref.shape[1]

    @pl.when(v == 0)
    def _():
        top_ref[...] = jnp.full_like(top_ref, -jnp.inf)
        sum_ref[...] = jnp.zeros_like(sum_ref)
        hit_ref[...] = jnp.zeros_like(hit_ref)

    def visit(head_ref, first):
        digits = rows_ref[:, D : D + EXTRA].astype(jnp.float32)
        label = digits[:, 0:1] * 65536.0 + digits[:, 1:2] * 256.0 + digits[:, 2:3]
        logits = jnp.dot(rows_ref[:, :D], head_ref[...], preferred_element_type=jnp.float32)
        lanes = lax.broadcasted_iota(jnp.int32, (1, 128), 1).astype(jnp.float32)
        label = label - first.astype(jnp.float32)
        slabs = [logits[:, c : c + 128] for c in range(0, tile, 128)]
        top = top_ref[...]
        high = functools.reduce(jnp.maximum, slabs, top)
        total = sum_ref[...] * jnp.exp(top - high)
        hit = hit_ref[...]
        for c, slab in enumerate(slabs):
            total = total + jnp.exp(slab - high)
            hit = hit + jnp.where(lanes + float(c * 128) == label, slab, 0.0)
        top_ref[...] = high
        sum_ref[...] = total
        hit_ref[...] = hit

    @pl.when(v < steps_each)
    def _():
        visit(own_ref, first_ref[0] + v * tile)

    @pl.when(v >= steps_each)
    def _():
        visit(other_ref, first_ref[1] + (v - steps_each) * tile)

    @pl.when(v == pl.num_programs(1) - 1)
    def _():
        top = top_ref[...]
        high = jnp.max(top, axis=1, keepdims=True)
        total = jnp.sum(sum_ref[...] * jnp.exp(top - high), axis=1, keepdims=True)
        hit = jnp.sum(hit_ref[...], axis=1, keepdims=True)
        lane = lax.broadcasted_iota(jnp.int32, top.shape, 1)
        both = jnp.where(lane == 0, high + jnp.log(total), hit)
        out_ref[...] = both.T[:8, :]


def vocabulary_stats(rows, own_head, other_head, firsts, tile_rows=512, tile=256):
    count = rows.shape[0]
    tile_rows = min(tile_rows, count)
    steps_each = own_head.shape[1] // tile
    return pl.pallas_call(
        functools.partial(logits_kernel, steps_each=steps_each),
        grid=(count // tile_rows, 2 * steps_each),
        in_specs=[
            pl.BlockSpec(memory_space=pltpu.SMEM),
            pl.BlockSpec((tile_rows, D + EXTRA), lambda r, v: (r, 0)),
            pl.BlockSpec((D, tile), lambda r, v: (0, jnp.minimum(v, steps_each - 1))),
            pl.BlockSpec((D, tile), lambda r, v: (0, jnp.maximum(v - steps_each, 0))),
        ],
        out_specs=pl.BlockSpec((8, tile_rows), lambda r, v: (0, r)),
        out_shape=jax.ShapeDtypeStruct((8, count), jnp.float32),
        scratch_shapes=[pltpu.VMEM((tile_rows, 128), jnp.float32)] * 3,
        cost_estimate=pl.CostEstimate(
            flops=2 * count * D * 2 * own_head.shape[1], bytes_accessed=count * D * 2, transcendentals=0
        ),
        compiler_params=pltpu.CompilerParams(vmem_limit_bytes=44 << 20),
        name="vocabulary_stats",
    )(firsts, rows, own_head, other_head)


def update_kernel(gap_ref, noise_ref, out_ref):
    rows = out_ref.shape[0]
    pairs = noise_ref.shape[0]
    for r in range(0, rows, 16):
        deep = min(16, rows - r)
        total = None
        for p in range(pairs):
            term = gap_ref[p] * noise_ref[p, r : r + 16, :].astype(jnp.float32)
            total = term if total is None else total + term
        out_ref[r : r + deep, :] = total[:deep]


def update(gap, noise, rows, tile=512):
    pairs, padded, _ = noise.shape
    return pl.pallas_call(
        update_kernel,
        grid=(D // tile,),
        in_specs=[
            pl.BlockSpec(memory_space=pltpu.SMEM),
            pl.BlockSpec((pairs, padded, tile), lambda c: (0, 0, c)),
        ],
        out_specs=pl.BlockSpec((rows, tile), lambda c: (0, c)),
        out_shape=jax.ShapeDtypeStruct((rows, D), jnp.float32),
        cost_estimate=pl.CostEstimate(
            flops=2 * pairs * rows * D, bytes_accessed=2 * pairs * padded * D, transcendentals=0
        ),
        compiler_params=pltpu.CompilerParams(vmem_limit_bytes=44 << 20),
        name="update",
    )(gap, noise)


def scattered_sum(partial, axes, shares):
    rows = partial.shape[0] // shares
    pieces = lax.all_to_all(partial.reshape(shares, rows, partial.shape[1]), axes, 0, 0)
    return jnp.sum(pieces.astype(jnp.float32), axis=0)


def joined(stats, axes, count):
    everyone = lax.all_to_all(jnp.broadcast_to(stats[None], (count,) + stats.shape), axes, 0, 0)
    level = everyone[:, 0]
    top = jnp.max(level, axis=0)
    level = top + jnp.log(jnp.sum(jnp.exp(level - top[None]), axis=0))
    return jnp.stack([level, jnp.sum(everyone[:, 1], axis=0)])


def local(hidden_units, residual, down_weight, norm_gain, head, labels, answer_start, seeds, signs):
    y_lo, x, core = lax.axis_index("y_lo"), lax.axis_index("x"), lax.axis_index("core")
    pop_at = (y_lo * lax.axis_size("x") + x) * 2 + core
    tp_at = lax.axis_index("z") * 2 + lax.axis_index("y_hi")
    tp_count = lax.axis_size("z") * 2
    pop_count = seeds.shape[0]
    chip_pairs = pop_count // 2
    tokens = hidden_units.shape[1]
    scored = tokens - SKIP
    share = scored // tp_count
    units = down_weight.shape[0]
    vocab = head.shape[1]
    noise_scale = 0.25 * FF ** (-0.5)
    swap = [(0, 1), (1, 0)]

    other_head = lax.ppermute(head, "core", swap)
    seed_terms = seeds * jnp.int32(1540483477)
    own_seed = lax.dynamic_index_in_dim(seed_terms, pop_at, 0, keepdims=False)
    start = (own_seed + tp_at * jnp.int32(units * D)).reshape(1)

    first_cols = 1024
    probe_a, base = probe_call(
        start, hidden_units[0], down_weight, 0, first_cols, 256, jnp.bfloat16, jnp.float32
    )
    (probe_b,) = probe_call(start, hidden_units[0], None, first_cols, D - first_cols, 256, jnp.bfloat16, None)
    base = scattered_sum(base, TP, tp_count)
    probe = jnp.concatenate([probe_a, probe_b], axis=1)
    probe = scattered_sum(probe, TP, tp_count)

    token_at = SKIP + tp_at * share
    pair_signs = lax.dynamic_slice_in_dim(signs, pop_at * 2, 2).astype(jnp.float32)
    own_residual = lax.dynamic_slice_in_dim(residual[0], token_at, share, 0).astype(jnp.float32)
    layer = (own_residual + base)[None] + pair_signs[:, None, None] * noise_scale * probe[None]
    mean_square = jnp.mean(layer * layer, axis=2, keepdims=True)
    normed = (layer * lax.rsqrt(mean_square + 1e-06) * norm_gain).astype(jnp.bfloat16)
    own_labels = lax.dynamic_slice_in_dim(labels[0], token_at, share, 0)
    places = jnp.arange(EXTRA, dtype=jnp.int32)[None, :]
    digits = (own_labels[:, None] >> jnp.clip(16 - 8 * places, 0, 16)) & 255
    digits = jnp.where(places < 3, digits, 0).astype(jnp.bfloat16)
    normed = jnp.concatenate([normed, jnp.broadcast_to(digits[None], (2, share, EXTRA))], axis=2)
    rows = lax.all_gather(normed.reshape(2 * share, D + EXTRA), SAME_CORE, axis=0, tiled=True)

    out_rows = FF // (pop_count * tp_count)
    own_first = (pop_at * tp_count + tp_at) * jnp.int32(out_rows * D)
    noise = regenerate(seed_terms + own_first, out_rows)

    own_vocab = (pop_at * tp_count + tp_at) * vocab
    other_vocab = ((pop_at + 1 - 2 * core) * tp_count + tp_at) * vocab
    stats = vocabulary_stats(rows, head, other_head, jnp.stack([own_vocab, other_vocab]))[:2]
    stats = joined(stats, TP, tp_count)
    stats = joined(stats, ("y_lo", "x"), chip_pairs)
    log_prob = (stats[1] - stats[0]).reshape(tp_count, chip_pairs, 2, share)
    positions = SKIP + jnp.arange(scored, dtype=jnp.int32).reshape(tp_count, 1, share)
    own_starts = lax.dynamic_index_in_dim(answer_start.reshape(chip_pairs, 2), core, 1, keepdims=False)
    mask = (positions >= own_starts[None, :, None]).astype(jnp.float32)
    own_fitness = jnp.sum(log_prob * mask[:, :, None, :], axis=(0, 3)) / (tokens - own_starts).astype(jnp.float32)[:, None]
    other_fitness = lax.ppermute(own_fitness, "core", swap)
    ordered = jnp.where(
        core == 0,
        jnp.stack([own_fitness, other_fitness], axis=1),
        jnp.stack([other_fitness, own_fitness], axis=1),
    )
    fitness = ordered.reshape(2 * pop_count)
    gap = jnp.sum((fitness * signs.astype(jnp.float32)).reshape(pop_count, 2), axis=1)
    return fitness, update(gap, noise, out_rows)


def solution(mesh):
    fine = Mesh(mesh.devices.reshape(2, 4, 2, 4, 2), ("y_lo", "x", "core", "z", "y_hi"))
    pop = ("y_lo", "x", "core")
    return jax.shard_map(
        local,
        mesh=fine,
        in_specs=(
            P(pop, None, TP),
            P(pop, None, None),
            P(TP, None),
            P(),
            P(None, pop + TP),
            P(pop, None),
            P(),
            P(),
            P(),
        ),
        out_specs=(P(), P(pop + TP, None)),
        check_vma=False,
    )
```

```python
import functools

import jax
import jax.numpy as jnp
from jax import lax
from jax.experimental import pallas as pl
from jax.experimental.pallas import tpu as pltpu
from jax.sharding import Mesh, PartitionSpec as P

FF = 18944
D = 3584
SKIP = 32
EXTRA = 128

MUL_A = 739982445
MUL_B = 695872825
SALT = 1013904223
SALT_MIXED = SALT ^ (SALT >> 15)
root_three = 1.7320508075688772

TP = ("z", "y_hi")
SAME_CORE = ("z", "y_hi", "y_lo", "x")


def shifted(hashed, places):
    return lax.shift_right_logical(hashed, jnp.full_like(hashed, places))


def noise_of(index):
    h = index ^ shifted(index, 15)
    h = h * jnp.int32(MUL_A)
    h = h ^ shifted(h, 12)
    h = h * jnp.int32(MUL_B)
    h = h ^ shifted(h, 30) ^ jnp.int32(SALT_MIXED)
    h = h * jnp.int32(MUL_A)
    h = h ^ shifted(h, 12)
    h = h * jnp.int32(MUL_B)
    bits = (h ^ shifted(h, 15)) & jnp.int32(16777215)
    return ((bits.astype(jnp.float32) - 8388607.5) * jnp.float32(root_three / 8388608.0)).astype(jnp.bfloat16)


def flat_index(rows, cols, width):
    return lax.broadcasted_iota(jnp.int32, (rows, cols), 0) * width + lax.broadcasted_iota(jnp.int32, (rows, cols), 1)


def probe_kernel(start_ref, hidden_ref, *refs, first_step, share, with_base):
    if with_base:
        left_ref, right_ref, probe_ref, base_ref = refs
    else:
        _, probe_ref = refs
    units = hidden_ref.shape[1]
    half = D // 2
    step = pl.program_id(0) + first_step
    lane = lax.broadcasted_iota(jnp.int32, (256, 256), 1)
    index = lax.broadcasted_iota(jnp.int32, (256, 256), 0) * D + jnp.where(lane < 128, lane, lane + (half - 128))
    at = start_ref[0] + step * 128
    total = None
    for k in range(0, units, 256):
        depth = min(256, units - k)
        noise = noise_of(index[:depth] + (at + k * D))
        part = jnp.dot(hidden_ref[SKIP:, k : k + depth], noise, preferred_element_type=jnp.float32)
        total = part if total is None else total + part
    for t in range(probe_ref.shape[0]):
        rows = slice(t * share, (t + 1) * share)
        probe_ref[t] = jnp.concatenate([total[rows, :128], total[rows, 128:]], axis=0).astype(probe_ref.dtype)
    if with_base:
        left = jnp.dot(hidden_ref[SKIP:, :], left_ref[...], preferred_element_type=jnp.float32)
        right = jnp.dot(hidden_ref[SKIP:, :], right_ref[...], preferred_element_type=jnp.float32)
        for t in range(base_ref.shape[0]):
            rows = slice(t * share, (t + 1) * share)
            base_ref[t] = jnp.concatenate([left[rows], right[rows]], axis=0).astype(base_ref.dtype)


def products(start, hidden, weight, shares, first_steps=2):
    tokens, units = hidden.shape
    share = (tokens - SKIP) // shares
    half = D // 2
    steps = half // 128
    probe_shape = jax.ShapeDtypeStruct((shares, 2 * share, half), jnp.bfloat16)
    scalar = pl.BlockSpec(memory_space=pltpu.SMEM)
    whole = pl.BlockSpec((tokens, units), lambda i: (0, 0))
    params = pltpu.CompilerParams(vmem_limit_bytes=56 << 20)

    def cost(count):
        return pl.CostEstimate(flops=units * count * 256 * 2000, bytes_accessed=units * count * 256, transcendentals=0)

    wide = half // first_steps
    probe, base = pl.pallas_call(
        functools.partial(probe_kernel, first_step=0, share=share, with_base=True),
        grid=(first_steps,),
        in_specs=[
            scalar,
            whole,
            pl.BlockSpec((units, wide), lambda i: (0, i)),
            pl.BlockSpec((units, wide), lambda i: (0, i + first_steps)),
        ],
        out_specs=[
            pl.BlockSpec((shares, 2 * share, 128), lambda i: (0, 0, i)),
            pl.BlockSpec((shares, 2 * share, wide), lambda i: (0, 0, i)),
        ],
        out_shape=[probe_shape, jax.ShapeDtypeStruct((shares, 2 * share, half), jnp.float32)],
        cost_estimate=cost(first_steps),
        compiler_params=params,
        name="base_and_probe",
    )(start, hidden, weight, weight)
    probe = pl.pallas_call(
        functools.partial(probe_kernel, first_step=first_steps, share=share, with_base=False),
        grid=(steps - first_steps,),
        in_specs=[scalar, whole, pl.BlockSpec(memory_space=pl.ANY)],
        out_specs=pl.BlockSpec((shares, 2 * share, 128), lambda i: (0, 0, i + first_steps)),
        out_shape=probe_shape,
        input_output_aliases={2: 0},
        cost_estimate=cost(steps - first_steps),
        compiler_params=params,
        name="probe",
    )(start, hidden, probe)
    return probe, base


def regenerate_kernel(start_ref, out_ref, *, width):
    at = start_ref[pl.program_id(0)]

    def rows16(r, _):
        first = pl.multiple_of(r * 16, 16)
        for c in range(0, D, width):
            out_ref[0, pl.ds(first, 16), c : c + width] = noise_of(flat_index(16, width, D) + (at + r * (16 * D) + c))
        return 0

    lax.fori_loop(0, out_ref.shape[1] // 16, rows16, 0)


def regenerate(starts, rows):
    pairs = starts.shape[0]
    padded = -(-rows // 16) * 16
    return pl.pallas_call(
        functools.partial(regenerate_kernel, width=512),
        grid=(pairs,),
        in_specs=[pl.BlockSpec(memory_space=pltpu.SMEM)],
        out_specs=pl.BlockSpec((1, padded, D), lambda p: (p, 0, 0)),
        out_shape=jax.ShapeDtypeStruct((pairs, padded, D), jnp.bfloat16),
        cost_estimate=pl.CostEstimate(
            flops=pairs * padded * D * 2000, bytes_accessed=pairs * padded * D * 2, transcendentals=0
        ),
        compiler_params=pltpu.CompilerParams(vmem_limit_bytes=44 << 20),
        name="regenerate",
    )(starts)


LOWEST = -1e30


def logits_kernel(first_ref, rows_ref, own_ref, other_ref, out_ref, top_ref, sum_ref, hit_ref, held_ref, *, chunk):
    v = pl.program_id(1)
    count, vocab = rows_ref.shape[0], own_ref.shape[1]
    lanes = lax.broadcasted_iota(jnp.int32, (1, 128), 1).astype(jnp.float32)

    def absorb(slot, r, first):
        some = pl.ds(r, chunk)
        digits = rows_ref[some, D : D + EXTRA].astype(jnp.float32)
        label = digits[:, 0:1] * 65536.0 + digits[:, 1:2] * 256.0 + digits[:, 2:3] - first.astype(jnp.float32)
        slabs = [held_ref[slot, some, c : c + 128] for c in range(0, vocab, 128)]
        top = top_ref[some, :]
        high = functools.reduce(jnp.maximum, slabs, top)
        total = sum_ref[some, :] * jnp.exp(top - high)
        hit = hit_ref[some, :]
        for c, slab in enumerate(slabs):
            total = total + jnp.exp(slab - high)
            hit = hit + jnp.where(lanes + float(c * 128) == label, slab, 0.0)
        top_ref[some, :] = high
        sum_ref[some, :] = total
        hit_ref[some, :] = hit

    def multiply(slot, r, head_ref):
        some = pl.ds(r, chunk)
        held_ref[slot, some, :] = jnp.dot(rows_ref[some, :D], head_ref[...], preferred_element_type=jnp.float32)

    @pl.when(v == 0)
    def _():
        top_ref[...] = jnp.full_like(top_ref, LOWEST)
        sum_ref[...] = jnp.zeros_like(sum_ref)
        hit_ref[...] = jnp.zeros_like(hit_ref)
        for r in range(0, count, chunk):
            multiply(0, r, own_ref)

    @pl.when(v == 1)
    def _():
        for r in range(0, count, chunk):
            multiply(1, r, other_ref)
            absorb(0, r, first_ref[0])
        for r in range(0, count, chunk):
            absorb(1, r, first_ref[1])
        top = top_ref[...]
        high = jnp.max(top, axis=1, keepdims=True)
        total = jnp.sum(sum_ref[...] * jnp.exp(top - high), axis=1, keepdims=True)
        hit = jnp.sum(hit_ref[...], axis=1, keepdims=True)
        lane = lax.broadcasted_iota(jnp.int32, top.shape, 1)
        both = jnp.where(lane == 0, high + jnp.log(total), hit)
        out_ref[...] = both.T[:8, :]


def vocabulary_stats(rows, own_head, other_head, firsts, tile_rows=512, chunk=256):
    count = rows.shape[0]
    tile_rows = min(tile_rows, count)
    vocab = own_head.shape[1]
    head_spec = pl.BlockSpec((D, vocab), lambda r, v: (0, 0), pipeline_mode=pl.Buffered(1))
    return pl.pallas_call(
        functools.partial(logits_kernel, chunk=min(chunk, tile_rows)),
        grid=(count // tile_rows, 2),
        in_specs=[
            pl.BlockSpec(memory_space=pltpu.SMEM),
            pl.BlockSpec((tile_rows, D + EXTRA), lambda r, v: (r, 0)),
            head_spec,
            head_spec,
        ],
        out_specs=pl.BlockSpec((8, tile_rows), lambda r, v: (0, r)),
        out_shape=jax.ShapeDtypeStruct((8, count), jnp.float32),
        scratch_shapes=[pltpu.VMEM((tile_rows, 128), jnp.float32)] * 3
        + [pltpu.VMEM((2, tile_rows, vocab), jnp.float32)],
        cost_estimate=pl.CostEstimate(
            flops=2 * count * D * 2 * vocab, bytes_accessed=count * D * 2, transcendentals=0
        ),
        compiler_params=pltpu.CompilerParams(vmem_limit_bytes=56 << 20),
        name="vocabulary_stats",
    )(firsts, rows, own_head, other_head)


def update_kernel(gap_ref, noise_ref, out_ref):
    rows = out_ref.shape[0]
    pairs = noise_ref.shape[0]
    for r in range(0, rows, 16):
        deep = min(16, rows - r)
        total = None
        for p in range(pairs):
            term = gap_ref[p] * noise_ref[p, r : r + 16, :].astype(jnp.float32)
            total = term if total is None else total + term
        out_ref[r : r + deep, :] = total[:deep]


def update(gap, noise, rows, tile=896):
    pairs, padded, _ = noise.shape
    return pl.pallas_call(
        update_kernel,
        grid=(D // tile,),
        in_specs=[
            pl.BlockSpec(memory_space=pltpu.SMEM),
            pl.BlockSpec((pairs, padded, tile), lambda c: (0, 0, c)),
        ],
        out_specs=pl.BlockSpec((rows, tile), lambda c: (0, c)),
        out_shape=jax.ShapeDtypeStruct((rows, D), jnp.float32),
        cost_estimate=pl.CostEstimate(
            flops=2 * pairs * rows * D, bytes_accessed=2 * pairs * padded * D, transcendentals=0
        ),
        compiler_params=pltpu.CompilerParams(vmem_limit_bytes=44 << 20),
        name="update",
    )(gap, noise)


def scattered_sum(partial, axes):
    pieces = lax.all_to_all(partial, axes, 0, 0)
    total = jnp.sum(pieces.astype(jnp.float32), axis=0)
    share = total.shape[0] // 2
    return jnp.concatenate([total[:share], total[share:]], axis=1)


def joined(stats, axes, count):
    everyone = lax.all_to_all(jnp.broadcast_to(stats[None], (count,) + stats.shape), axes, 0, 0)
    level = everyone[:, 0]
    top = jnp.max(level, axis=0)
    level = top + jnp.log(jnp.sum(jnp.exp(level - top[None]), axis=0))
    return jnp.stack([level, jnp.sum(everyone[:, 1], axis=0)])


def local(hidden_units, residual, down_weight, norm_gain, head, labels, answer_start, seeds, signs):
    y_lo, x, core = lax.axis_index("y_lo"), lax.axis_index("x"), lax.axis_index("core")
    pop_at = (y_lo * lax.axis_size("x") + x) * 2 + core
    tp_at = lax.axis_index("z") * 2 + lax.axis_index("y_hi")
    tp_count = lax.axis_size("z") * 2
    pop_count = seeds.shape[0]
    chip_pairs = pop_count // 2
    tokens = hidden_units.shape[1]
    scored = tokens - SKIP
    share = scored // tp_count
    units = down_weight.shape[0]
    vocab = head.shape[1]
    noise_scale = 0.25 * FF ** (-0.5)
    swap = [(0, 1), (1, 0)]

    other_head = lax.ppermute(head, "core", swap)
    seed_terms = seeds * jnp.int32(1540483477)
    own_seed = lax.dynamic_index_in_dim(seed_terms, pop_at, 0, keepdims=False)
    start = (own_seed + tp_at * jnp.int32(units * D)).reshape(1)

    probe, base = products(start, hidden_units[0], down_weight, tp_count)
    base = scattered_sum(base, TP)
    probe = scattered_sum(probe, TP)

    token_at = SKIP + tp_at * share
    pair_signs = lax.dynamic_slice_in_dim(signs, pop_at * 2, 2).astype(jnp.float32)
    own_residual = lax.dynamic_slice_in_dim(residual[0], token_at, share, 0).astype(jnp.float32)
    layer = (own_residual + base)[None] + pair_signs[:, None, None] * noise_scale * probe[None]
    mean_square = jnp.mean(layer * layer, axis=2, keepdims=True)
    normed = (layer * lax.rsqrt(mean_square + 1e-06) * norm_gain).astype(jnp.bfloat16)
    own_labels = lax.dynamic_slice_in_dim(labels[0], token_at, share, 0)
    places = jnp.arange(EXTRA, dtype=jnp.int32)[None, :]
    digits = (own_labels[:, None] >> jnp.clip(16 - 8 * places, 0, 16)) & 255
    digits = jnp.where(places < 3, digits, 0).astype(jnp.bfloat16)
    normed = jnp.concatenate([normed, jnp.broadcast_to(digits[None], (2, share, EXTRA))], axis=2)
    rows = lax.all_gather(normed.reshape(2 * share, D + EXTRA), SAME_CORE, axis=0, tiled=True)

    out_rows = FF // (pop_count * tp_count)
    own_first = (pop_at * tp_count + tp_at) * jnp.int32(out_rows * D)
    noise = regenerate(seed_terms + own_first, out_rows)

    own_vocab = (pop_at * tp_count + tp_at) * vocab
    other_vocab = ((pop_at + 1 - 2 * core) * tp_count + tp_at) * vocab
    stats = vocabulary_stats(rows, head, other_head, jnp.stack([own_vocab, other_vocab]))[:2]
    stats = joined(stats, TP, tp_count)
    stats = joined(stats, ("y_lo", "x"), chip_pairs)
    log_prob = (stats[1] - stats[0]).reshape(tp_count, chip_pairs, 2, share)
    positions = SKIP + jnp.arange(scored, dtype=jnp.int32).reshape(tp_count, 1, share)
    own_starts = lax.dynamic_index_in_dim(answer_start.reshape(chip_pairs, 2), core, 1, keepdims=False)
    mask = (positions >= own_starts[None, :, None]).astype(jnp.float32)
    own_fitness = jnp.sum(log_prob * mask[:, :, None, :], axis=(0, 3)) / (tokens - own_starts).astype(jnp.float32)[:, None]
    other_fitness = lax.ppermute(own_fitness, "core", swap)
    ordered = jnp.where(
        core == 0,
        jnp.stack([own_fitness, other_fitness], axis=1),
        jnp.stack([other_fitness, own_fitness], axis=1),
    )
    fitness = ordered.reshape(2 * pop_count)
    gap = jnp.sum((fitness * signs.astype(jnp.float32)).reshape(pop_count, 2), axis=1)
    return fitness, update(gap, noise, out_rows)


def solution(mesh):
    fine = Mesh(mesh.devices.reshape(2, 4, 2, 4, 2), ("y_lo", "x", "core", "z", "y_hi"))
    pop = ("y_lo", "x", "core")
    return jax.shard_map(
        local,
        mesh=fine,
        in_specs=(
            P(pop, None, TP),
            P(pop, None, None),
            P(TP, None),
            P(),
            P(None, pop + TP),
            P(pop, None),
            P(),
            P(),
            P(),
        ),
        out_specs=(P(), P(pop + TP, None)),
        check_vma=False,
    )
```

```python
import functools

import jax
import jax.numpy as jnp
from jax import lax
from jax.experimental import pallas as pl
from jax.experimental.pallas import tpu as pltpu
from jax.sharding import Mesh, PartitionSpec as P

FF = 18944
D = 3584
SKIP = 32
EXTRA = 128

MUL_A = 739982445
MUL_B = 695872825
SALT = 1013904223
SALT_MIXED = SALT ^ (SALT >> 15)
root_three = 1.7320508075688772

TP = ("z", "y_hi")
SAME_CORE = ("z", "y_hi", "y_lo", "x")


def shifted(hashed, places):
    return lax.shift_right_logical(hashed, jnp.full_like(hashed, places))


def noise_of(index):
    h = index ^ shifted(index, 15)
    h = h * jnp.int32(MUL_A)
    h = h ^ shifted(h, 12)
    h = h * jnp.int32(MUL_B)
    h = h ^ shifted(h, 30) ^ jnp.int32(SALT_MIXED)
    h = h * jnp.int32(MUL_A)
    h = h ^ shifted(h, 12)
    h = h * jnp.int32(MUL_B)
    bits = (h ^ shifted(h, 15)) & jnp.int32(16777215)
    return ((bits.astype(jnp.float32) - 8388607.5) * jnp.float32(root_three / 8388608.0)).astype(jnp.bfloat16)


def flat_index(rows, cols, width):
    return lax.broadcasted_iota(jnp.int32, (rows, cols), 0) * width + lax.broadcasted_iota(jnp.int32, (rows, cols), 1)


def places():
    pop_at = (lax.axis_index("y_lo") * lax.axis_size("x") + lax.axis_index("x")) * 2 + lax.axis_index("core")
    return pop_at, lax.axis_index("z") * 2 + lax.axis_index("y_hi")


def probe_step(seeds_ref, hidden_ref, step):
    units = hidden_ref.shape[1]
    half = D // 2
    lane = lax.broadcasted_iota(jnp.int32, (256, 256), 1)
    index = lax.broadcasted_iota(jnp.int32, (256, 256), 0) * D + jnp.where(lane < 128, lane, lane + (half - 128))
    pop_at, tp_at = places()
    at = seeds_ref[pop_at] * jnp.int32(1540483477) + tp_at * jnp.int32(units * D) + step * 128
    total = None
    for k in range(0, units, 256):
        depth = min(256, units - k)
        noise = noise_of(index[:depth] + (at + k * D))
        part = jnp.dot(hidden_ref[SKIP:, k : k + depth], noise, preferred_element_type=jnp.float32)
        total = part if total is None else total + part
    return total[:, :128], total[:, 128:]


def put_shares(ref, cols, left, right):
    share = ref.shape[1] // 2
    for t in range(ref.shape[0]):
        rows = slice(t * share, (t + 1) * share)
        ref[t, :, cols] = jnp.concatenate([left[rows], right[rows]], axis=0).astype(ref.dtype)


def first_kernel(seeds_ref, hidden_ref, weight_hbm, probe_ref, base_ref, weight_ref, sems, *, steps):
    half = D // 2
    wide = half // 2
    copies = []
    for c in range(4):
        cols = slice((c % 2) * half + (c // 2) * wide, (c % 2) * half + (c // 2 + 1) * wide)
        copies.append(pltpu.make_async_copy(weight_hbm.at[:, cols], weight_ref.at[c], sems.at[c]))
        copies[-1].start()
    for step in range(steps):
        put_shares(probe_ref, slice(step * 128, step * 128 + 128), *probe_step(seeds_ref, hidden_ref, step))
        if step + 2 < steps:
            continue
        c = 2 * (step + 2 - steps)
        sides = []
        for side in (c, c + 1):
            copies[side].wait()
            sides.append(jnp.dot(hidden_ref[SKIP:, :], weight_ref[side], preferred_element_type=jnp.float32))
        put_shares(base_ref, slice((c // 2) * wide, (c // 2 + 1) * wide), *sides)


def rest_kernel(seeds_ref, hidden_ref, _, probe_ref, *, first_step):
    put_shares(probe_ref, slice(None), *probe_step(seeds_ref, hidden_ref, pl.program_id(0) + first_step))


def products(seeds, hidden, weight, shares, first_steps=2):
    tokens, units = hidden.shape
    share = (tokens - SKIP) // shares
    half = D // 2
    steps = half // 128
    probe_shape = jax.ShapeDtypeStruct((shares, 2 * share, half), jnp.bfloat16)
    base_shape = jax.ShapeDtypeStruct((shares, 2 * share, half), jnp.float32)
    scalar = pl.BlockSpec(memory_space=pltpu.SMEM)
    whole = pl.BlockSpec((tokens, units), lambda i: (0, 0))
    params = pltpu.CompilerParams(vmem_limit_bytes=44 << 20)

    def cost(count):
        return pl.CostEstimate(flops=units * count * 256 * 2000, bytes_accessed=units * count * 256, transcendentals=0)

    probe, base = pl.pallas_call(
        functools.partial(first_kernel, steps=first_steps),
        grid=(1,),
        in_specs=[scalar, whole, pl.BlockSpec(memory_space=pl.ANY)],
        out_specs=[
            pl.BlockSpec((shares, 2 * share, first_steps * 128), lambda i: (0, 0, 0)),
            pl.BlockSpec((shares, 2 * share, half), lambda i: (0, 0, 0)),
        ],
        out_shape=[probe_shape, base_shape],
        scratch_shapes=[pltpu.VMEM((4, units, half // 2), jnp.bfloat16), pltpu.SemaphoreType.DMA((4,))],
        cost_estimate=cost(first_steps),
        compiler_params=params,
        name="base_and_probe",
    )(seeds, hidden, weight)
    probe = pl.pallas_call(
        functools.partial(rest_kernel, first_step=first_steps),
        grid=(steps - first_steps,),
        in_specs=[scalar, whole, pl.BlockSpec(memory_space=pl.ANY)],
        out_specs=pl.BlockSpec((shares, 2 * share, 128), lambda i: (0, 0, i + first_steps)),
        out_shape=probe_shape,
        input_output_aliases={2: 0},
        cost_estimate=cost(steps - first_steps),
        compiler_params=params,
        name="probe",
    )(seeds, hidden, probe)
    return probe, base


def regenerate_kernel(seeds_ref, out_ref, *, width, out_rows):
    pop_at, tp_at = places()
    pair = pl.program_id(0)
    at = seeds_ref[pair] * jnp.int32(1540483477) + (pop_at * lax.axis_size("z") * 2 + tp_at) * jnp.int32(out_rows * D)

    def rows16(r, _):
        first = pl.multiple_of(r * 16, 16)
        for c in range(0, D, width):
            out_ref[0, pl.ds(first, 16), c : c + width] = noise_of(
                flat_index(16, width, D) + (at + r * (16 * D) + c)
            )
        return 0

    lax.fori_loop(0, out_ref.shape[1] // 16, rows16, 0)


def regenerate(seeds, rows):
    pairs = seeds.shape[0]
    padded = -(-rows // 16) * 16
    return pl.pallas_call(
        functools.partial(regenerate_kernel, width=512, out_rows=rows),
        grid=(pairs,),
        in_specs=[pl.BlockSpec(memory_space=pltpu.SMEM)],
        out_specs=pl.BlockSpec((1, padded, D), lambda p: (p, 0, 0)),
        out_shape=jax.ShapeDtypeStruct((pairs, padded, D), jnp.bfloat16),
        cost_estimate=pl.CostEstimate(
            flops=pairs * padded * D * 2000, bytes_accessed=pairs * padded * D * 2, transcendentals=0
        ),
        compiler_params=pltpu.CompilerParams(vmem_limit_bytes=50 << 20),
        name="regenerate",
    )(seeds)


def logits_kernel(
    first_ref, rows_hbm, own_hbm, other_ref, out_ref, rows_ref, own_ref, held_ref, stats_ref, sems, own_sem
):
    slots, chunk, _ = rows_ref.shape
    chunks = rows_hbm.shape[0] // chunk
    vocab = own_ref.shape[1]
    lanes = lax.broadcasted_iota(jnp.int32, (1, 128), 1).astype(jnp.float32)

    def fetch(i):
        return pltpu.make_async_copy(
            rows_hbm.at[pl.ds(i * chunk, chunk), :], rows_ref.at[i % slots], sems.at[i % slots]
        )

    def multiply(i):
        rows = rows_ref[i % slots, :, :D]
        held_ref[i % 2, :, vocab:] = jnp.dot(rows, other_ref[...], preferred_element_type=jnp.float32)
        if i == 0:
            own.wait()
        held_ref[i % 2, :, :vocab] = jnp.dot(rows, own_ref[...], preferred_element_type=jnp.float32)

    def absorb(i):
        slot = i % 2
        high = held_ref[slot, :, :128]
        for c in range(128, 2 * vocab, 128):
            high = jnp.maximum(high, held_ref[slot, :, c : c + 128])
        high = jnp.broadcast_to(jnp.max(high, axis=1, keepdims=True), (chunk, 128))
        digits = rows_ref[i % slots, :, D : D + EXTRA].astype(jnp.float32)
        label = digits[:, 0:1] * 65536.0 + digits[:, 1:2] * 256.0 + digits[:, 2:3]
        label = [jnp.broadcast_to(label - first_ref[h].astype(jnp.float32), (chunk, 128)) for h in range(2)]
        total = jnp.zeros((chunk, 128), jnp.float32)
        hit = jnp.zeros((chunk, 128), jnp.float32)
        for c in range(0, 2 * vocab, 128):
            slab = held_ref[slot, :, c : c + 128]
            total = total + jnp.exp(slab - high)
            hit = jnp.where(lanes + float(c % vocab) == label[c // vocab], slab, hit)
        total = jnp.sum(total, axis=1, keepdims=True)
        hit = jnp.sum(hit, axis=1, keepdims=True)
        lane = lax.broadcasted_iota(jnp.int32, (chunk, 128), 1)
        stats_ref[i * chunk : (i + 1) * chunk, :] = jnp.where(lane == 0, high + jnp.log(total), hit)

    fetch(0).start()
    own = pltpu.make_async_copy(own_hbm, own_ref, own_sem)
    own.start()
    for i in range(1, min(slots - 1, chunks)):
        fetch(i).start()
    for i in range(chunks):
        fetch(i).wait()
        multiply(i)
        if i:
            absorb(i - 1)
        if i + slots - 1 < chunks:
            fetch(i + slots - 1).start()
    absorb(chunks - 1)
    out_ref[...] = stats_ref[...].T[:8, :]


def vocabulary_stats(rows, own_head, other_head, firsts, chunk=256, slots=4):
    count = rows.shape[0]
    vocab = own_head.shape[1]
    return pl.pallas_call(
        logits_kernel,
        in_specs=[
            pl.BlockSpec(memory_space=pltpu.SMEM),
            pl.BlockSpec(memory_space=pl.ANY),
            pl.BlockSpec(memory_space=pl.ANY),
            pl.BlockSpec(memory_space=pltpu.VMEM),
        ],
        out_specs=pl.BlockSpec(memory_space=pltpu.VMEM),
        out_shape=jax.ShapeDtypeStruct((8, count), jnp.float32),
        scratch_shapes=[
            pltpu.VMEM((slots, chunk, D + EXTRA), jnp.bfloat16),
            pltpu.VMEM((D, vocab), jnp.bfloat16),
            pltpu.VMEM((2, chunk, 2 * vocab), jnp.float32),
            pltpu.VMEM((count, 128), jnp.float32),
            pltpu.SemaphoreType.DMA((slots,)),
            pltpu.SemaphoreType.DMA,
        ],
        cost_estimate=pl.CostEstimate(
            flops=2 * count * D * 2 * vocab, bytes_accessed=count * D * 2, transcendentals=0
        ),
        compiler_params=pltpu.CompilerParams(vmem_limit_bytes=54 << 20),
        name="vocabulary_stats",
    )(firsts, rows, own_head, other_head)


def update_kernel(gap_ref, noise_ref, out_ref):
    rows = out_ref.shape[0]
    pairs = noise_ref.shape[0]
    for r in range(0, rows, 16):
        deep = min(16, rows - r)
        total = None
        for p in range(pairs):
            term = gap_ref[p] * noise_ref[p, r : r + 16, :].astype(jnp.float32)
            total = term if total is None else total + term
        out_ref[r : r + deep, :] = total[:deep]


def update(gap, noise, rows, tile=896):
    pairs, padded, _ = noise.shape
    return pl.pallas_call(
        update_kernel,
        grid=(D // tile,),
        in_specs=[
            pl.BlockSpec(memory_space=pltpu.SMEM),
            pl.BlockSpec((pairs, padded, tile), lambda c: (0, 0, c)),
        ],
        out_specs=pl.BlockSpec((rows, tile), lambda c: (0, c)),
        out_shape=jax.ShapeDtypeStruct((rows, D), jnp.float32),
        cost_estimate=pl.CostEstimate(
            flops=2 * pairs * rows * D, bytes_accessed=2 * pairs * padded * D, transcendentals=0
        ),
        compiler_params=pltpu.CompilerParams(vmem_limit_bytes=44 << 20),
        name="update",
    )(gap, noise)


def scattered_sum(partial, axes):
    pieces = lax.all_to_all(partial, axes, 0, 0)
    total = jnp.sum(pieces.astype(jnp.float32), axis=0)
    share = total.shape[0] // 2
    return jnp.concatenate([total[:share], total[share:]], axis=1)


def joined(stats, axes, count):
    everyone = lax.all_to_all(jnp.broadcast_to(stats[None], (count,) + stats.shape), axes, 0, 0)
    level = everyone[:, 0]
    top = jnp.max(level, axis=0)
    level = top + jnp.log(jnp.sum(jnp.exp(level - top[None]), axis=0))
    return jnp.stack([level, jnp.sum(everyone[:, 1], axis=0)])


def local(hidden_units, residual, down_weight, norm_gain, head, labels, answer_start, seeds, signs):
    core = lax.axis_index("core")
    pop_at, tp_at = places()
    tp_count = lax.axis_size("z") * 2
    pop_count = seeds.shape[0]
    chip_pairs = pop_count // 2
    tokens = hidden_units.shape[1]
    scored = tokens - SKIP
    share = scored // tp_count
    vocab = head.shape[1]
    noise_scale = 0.25 * FF ** (-0.5)
    swap = [(0, 1), (1, 0)]

    other_head = lax.ppermute(head, "core", swap)

    probe, base = products(seeds, hidden_units[0], down_weight, tp_count)
    base = scattered_sum(base, TP)
    probe, base = lax.optimization_barrier((probe, base))
    probe = scattered_sum(probe, TP)

    token_at = SKIP + tp_at * share
    pair_signs = lax.dynamic_slice_in_dim(signs, pop_at * 2, 2).astype(jnp.float32)
    own_residual = lax.dynamic_slice_in_dim(residual[0], token_at, share, 0).astype(jnp.float32)
    layer = (own_residual + base)[None] + pair_signs[:, None, None] * noise_scale * probe[None]
    mean_square = jnp.mean(layer * layer, axis=2, keepdims=True)
    normed = (layer * lax.rsqrt(mean_square + 1e-06) * norm_gain).astype(jnp.bfloat16)
    own_labels = lax.dynamic_slice_in_dim(labels[0], token_at, share, 0)
    slots = jnp.arange(EXTRA, dtype=jnp.int32)[None, :]
    digits = (own_labels[:, None] >> jnp.clip(16 - 8 * slots, 0, 16)) & 255
    digits = jnp.where(slots < 3, digits, 0).astype(jnp.bfloat16)
    normed = jnp.concatenate([normed, jnp.broadcast_to(digits[None], (2, share, EXTRA))], axis=2)

    out_rows = FF // (pop_count * tp_count)
    later_seeds, normed = lax.optimization_barrier((seeds, normed))
    rows = lax.all_gather(normed.reshape(2 * share, D + EXTRA), SAME_CORE, axis=0, tiled=True)
    noise = regenerate(later_seeds, out_rows)

    own_vocab = (pop_at * tp_count + tp_at) * vocab
    other_vocab = ((pop_at + 1 - 2 * core) * tp_count + tp_at) * vocab
    firsts, noise = lax.optimization_barrier((jnp.stack([own_vocab, other_vocab]), noise))
    stats = vocabulary_stats(rows, head, other_head, firsts)[:2]
    stats = joined(stats, TP, tp_count)
    stats = joined(stats, ("y_lo", "x"), chip_pairs)
    log_prob = (stats[1] - stats[0]).reshape(tp_count, chip_pairs, 2, share)
    positions = SKIP + jnp.arange(scored, dtype=jnp.int32).reshape(tp_count, 1, share)
    own_starts = lax.dynamic_index_in_dim(answer_start.reshape(chip_pairs, 2), core, 1, keepdims=False)
    mask = (positions >= own_starts[None, :, None]).astype(jnp.float32)
    own_fitness = jnp.sum(log_prob * mask[:, :, None, :], axis=(0, 3)) / (tokens - own_starts).astype(jnp.float32)[:, None]
    other_fitness = lax.ppermute(own_fitness, "core", swap)
    ordered = jnp.where(
        core == 0,
        jnp.stack([own_fitness, other_fitness], axis=1),
        jnp.stack([other_fitness, own_fitness], axis=1),
    )
    fitness = ordered.reshape(2 * pop_count)
    gap = jnp.sum((fitness * signs.astype(jnp.float32)).reshape(pop_count, 2), axis=1)
    return fitness, update(gap, noise, out_rows)


def solution(mesh):
    fine = Mesh(mesh.devices.reshape(2, 4, 2, 4, 2), ("y_lo", "x", "core", "z", "y_hi"))
    pop = ("y_lo", "x", "core")
    return jax.shard_map(
        local,
        mesh=fine,
        in_specs=(
            P(pop, None, TP),
            P(pop, None, None),
            P(TP, None),
            P(),
            P(None, pop + TP),
            P(pop, None),
            P(),
            P(),
            P(),
        ),
        out_specs=(P(), P(pop + TP, None)),
        check_vma=False,
    )
```

```python
import functools

import jax
import jax.numpy as jnp
from jax import lax
from jax.experimental import pallas as pl
from jax.experimental.pallas import tpu as pltpu
from jax.sharding import Mesh, PartitionSpec as P

FF = 18944
D = 3584
SKIP = 32
EXTRA = 128

MUL_A = 739982445
MUL_B = 695872825
SALT = 1013904223
SALT_MIXED = SALT ^ (SALT >> 15)
root_three = 1.7320508075688772

TP = ("z", "y_hi")
SAME_CORE = ("z", "y_hi", "y_lo", "x")


def shifted(hashed, places):
    return lax.shift_right_logical(hashed, jnp.full_like(hashed, places))


def noise_of(index):
    h = index ^ shifted(index, 15)
    h = h * jnp.int32(MUL_A)
    h = h ^ shifted(h, 12)
    h = h * jnp.int32(MUL_B)
    h = h ^ shifted(h, 30) ^ jnp.int32(SALT_MIXED)
    h = h * jnp.int32(MUL_A)
    h = h ^ shifted(h, 12)
    h = h * jnp.int32(MUL_B)
    bits = (h ^ shifted(h, 15)) & jnp.int32(16777215)
    return ((bits.astype(jnp.float32) - 8388607.5) * jnp.float32(root_three / 8388608.0)).astype(jnp.bfloat16)


def flat_index(rows, cols, width):
    return lax.broadcasted_iota(jnp.int32, (rows, cols), 0) * width + lax.broadcasted_iota(jnp.int32, (rows, cols), 1)


def places():
    pop_at = (lax.axis_index("y_lo") * lax.axis_size("x") + lax.axis_index("x")) * 2 + lax.axis_index("core")
    return pop_at, lax.axis_index("z") * 2 + lax.axis_index("y_hi")


def probe_step(seeds_ref, hidden_ref, step):
    units = hidden_ref.shape[1]
    half = D // 2
    lane = lax.broadcasted_iota(jnp.int32, (256, 256), 1)
    index = lax.broadcasted_iota(jnp.int32, (256, 256), 0) * D + jnp.where(lane < 128, lane, lane + (half - 128))
    pop_at, tp_at = places()
    at = seeds_ref[pop_at] * jnp.int32(1540483477) + tp_at * jnp.int32(units * D) + step * 128
    total = None
    for k in range(0, units, 256):
        depth = min(256, units - k)
        noise = noise_of(index[:depth] + (at + k * D))
        part = jnp.dot(hidden_ref[SKIP:, k : k + depth], noise, preferred_element_type=jnp.float32)
        total = part if total is None else total + part
    return total[:, :128], total[:, 128:]


def put_shares(ref, cols, left, right):
    share = ref.shape[1] // 2
    for t in range(ref.shape[0]):
        rows = slice(t * share, (t + 1) * share)
        ref[t, :, cols] = jnp.concatenate([left[rows], right[rows]], axis=0).astype(ref.dtype)


def first_kernel(seeds_ref, hidden_ref, weight_hbm, probe_ref, base_ref, weight_ref, sems, *, steps):
    half = D // 2
    wide = half // 2
    copies = []
    for c in range(4):
        cols = slice((c % 2) * half + (c // 2) * wide, (c % 2) * half + (c // 2 + 1) * wide)
        copies.append(pltpu.make_async_copy(weight_hbm.at[:, cols], weight_ref.at[c], sems.at[c]))
        copies[-1].start()
    for step in range(steps):
        c = 2 * (step + 2 - steps)
        if c >= 0:
            copies[c].wait()
            copies[c + 1].wait()
        probe_sides = probe_step(seeds_ref, hidden_ref, step)
        if c >= 0:
            sides = [
                jnp.dot(hidden_ref[SKIP:, :], weight_ref[side], preferred_element_type=jnp.float32)
                for side in (c, c + 1)
            ]
            put_shares(base_ref, slice((c // 2) * wide, (c // 2 + 1) * wide), *sides)
        put_shares(probe_ref, slice(step * 128, step * 128 + 128), *probe_sides)


def rest_kernel(seeds_ref, hidden_ref, _, probe_ref, *, first_step):
    put_shares(probe_ref, slice(None), *probe_step(seeds_ref, hidden_ref, pl.program_id(0) + first_step))


def products(seeds, hidden, weight, shares, first_steps=4):
    tokens, units = hidden.shape
    share = (tokens - SKIP) // shares
    half = D // 2
    steps = half // 128
    probe_shape = jax.ShapeDtypeStruct((shares, 2 * share, half), jnp.bfloat16)
    base_shape = jax.ShapeDtypeStruct((shares, 2 * share, half), jnp.float32)
    scalar = pl.BlockSpec(memory_space=pltpu.SMEM)
    whole = pl.BlockSpec((tokens, units), lambda i: (0, 0))
    params = pltpu.CompilerParams(vmem_limit_bytes=44 << 20)

    def cost(count):
        return pl.CostEstimate(flops=units * count * 256 * 2000, bytes_accessed=units * count * 256, transcendentals=0)

    probe, base = pl.pallas_call(
        functools.partial(first_kernel, steps=first_steps),
        grid=(1,),
        in_specs=[scalar, whole, pl.BlockSpec(memory_space=pl.ANY)],
        out_specs=[
            pl.BlockSpec((shares, 2 * share, first_steps * 128), lambda i: (0, 0, 0)),
            pl.BlockSpec((shares, 2 * share, half), lambda i: (0, 0, 0)),
        ],
        out_shape=[probe_shape, base_shape],
        scratch_shapes=[pltpu.VMEM((4, units, half // 2), jnp.bfloat16), pltpu.SemaphoreType.DMA((4,))],
        cost_estimate=cost(first_steps),
        compiler_params=params,
        name="base_and_probe",
    )(seeds, hidden, weight)
    probe = pl.pallas_call(
        functools.partial(rest_kernel, first_step=first_steps),
        grid=(steps - first_steps,),
        in_specs=[scalar, whole, pl.BlockSpec(memory_space=pl.ANY)],
        out_specs=pl.BlockSpec((shares, 2 * share, 128), lambda i: (0, 0, i + first_steps)),
        out_shape=probe_shape,
        input_output_aliases={2: 0},
        cost_estimate=cost(steps - first_steps),
        compiler_params=params,
        name="probe",
    )(seeds, hidden, probe)
    return probe, base


def regenerate_kernel(seeds_ref, out_ref, *, width, out_rows):
    pop_at, tp_at = places()
    pair = pl.program_id(0)
    at = seeds_ref[pair] * jnp.int32(1540483477) + (pop_at * lax.axis_size("z") * 2 + tp_at) * jnp.int32(out_rows * D)

    def rows16(r, _):
        first = pl.multiple_of(r * 16, 16)
        for c in range(0, D, width):
            out_ref[c // width, 0, pl.ds(first, 16), :] = noise_of(
                flat_index(16, width, D) + (at + r * (16 * D) + c)
            )
        return 0

    lax.fori_loop(0, out_ref.shape[2] // 16, rows16, 0)


def regenerate(seeds, rows, width=512):
    pairs = seeds.shape[0]
    padded = -(-rows // 16) * 16
    return pl.pallas_call(
        functools.partial(regenerate_kernel, width=width, out_rows=rows),
        grid=(pairs,),
        in_specs=[pl.BlockSpec(memory_space=pltpu.SMEM)],
        out_specs=pl.BlockSpec((D // width, 1, padded, width), lambda p: (0, p, 0, 0)),
        out_shape=jax.ShapeDtypeStruct((D // width, pairs, padded, width), jnp.bfloat16),
        cost_estimate=pl.CostEstimate(
            flops=pairs * padded * D * 2000, bytes_accessed=pairs * padded * D * 2, transcendentals=0
        ),
        compiler_params=pltpu.CompilerParams(vmem_limit_bytes=50 << 20),
        name="regenerate",
    )(seeds)


def logits_kernel(
    first_ref, rows_hbm, own_hbm, other_hbm, out_ref, rows_ref, own_ref, other_ref, held_ref, stats_ref, sems, head_sems
):
    slots, chunk, _ = rows_ref.shape
    chunks = rows_hbm.shape[0] // chunk
    vocab = own_ref.shape[1]
    lanes = lax.broadcasted_iota(jnp.int32, (1, 128), 1).astype(jnp.float32)

    def fetch(i):
        return pltpu.make_async_copy(
            rows_hbm.at[pl.ds(i * chunk, chunk), :], rows_ref.at[i % slots], sems.at[i % slots]
        )

    early = vocab // 3
    heads = [
        pltpu.make_async_copy(own_hbm.at[:, :early], own_ref.at[:, :early], head_sems.at[0]),
        pltpu.make_async_copy(own_hbm.at[:, early:], own_ref.at[:, early:], head_sems.at[1]),
        pltpu.make_async_copy(other_hbm, other_ref, head_sems.at[2]),
    ]

    def multiply(i):
        rows = rows_ref[i % slots, :, :D]
        if i == 0:
            for copy, ref, cols, at in (
                (heads[0], own_ref, slice(0, early), 0),
                (heads[1], own_ref, slice(early, vocab), early),
                (heads[2], other_ref, slice(0, vocab), vocab),
            ):
                copy.wait()
                made = jnp.dot(rows, ref[:, cols], preferred_element_type=jnp.float32)
                held_ref[0, :, at : at + made.shape[1]] = made
        else:
            held_ref[i % 2, :, :vocab] = jnp.dot(rows, own_ref[...], preferred_element_type=jnp.float32)
            held_ref[i % 2, :, vocab:] = jnp.dot(rows, other_ref[...], preferred_element_type=jnp.float32)

    def absorb(i):
        slot = i % 2
        high = held_ref[slot, :, :128]
        for c in range(128, 2 * vocab, 128):
            high = jnp.maximum(high, held_ref[slot, :, c : c + 128])
        high = jnp.broadcast_to(jnp.max(high, axis=1, keepdims=True), (chunk, 128))
        digits = rows_ref[i % slots, :, D : D + EXTRA].astype(jnp.float32)
        label = digits[:, 0:1] * 65536.0 + digits[:, 1:2] * 256.0 + digits[:, 2:3]
        label = [jnp.broadcast_to(label - first_ref[h].astype(jnp.float32), (chunk, 128)) for h in range(2)]
        total = jnp.zeros((chunk, 128), jnp.float32)
        hit = jnp.zeros((chunk, 128), jnp.float32)
        for c in range(0, 2 * vocab, 128):
            slab = held_ref[slot, :, c : c + 128]
            total = total + jnp.exp(slab - high)
            hit = jnp.where(lanes + float(c % vocab) == label[c // vocab], slab, hit)
        total = jnp.sum(total, axis=1, keepdims=True)
        hit = jnp.sum(hit, axis=1, keepdims=True)
        lane = lax.broadcasted_iota(jnp.int32, (chunk, 128), 1)
        stats_ref[i * chunk : (i + 1) * chunk, :] = jnp.where(lane == 0, high + jnp.log(total), hit)

    fetch(0).start()
    for copy in heads:
        copy.start()
    for i in range(1, min(slots - 1, chunks)):
        fetch(i).start()
    for i in range(chunks):
        fetch(i).wait()
        multiply(i)
        if i:
            absorb(i - 1)
        if i + slots - 1 < chunks:
            fetch(i + slots - 1).start()
    absorb(chunks - 1)
    both = stats_ref[...].T[:2, :]
    for t in range(out_ref.shape[0]):
        out_ref[t] = both


def vocabulary_stats(rows, own_head, other_head, firsts, copies, chunk=256, slots=4):
    count = rows.shape[0]
    vocab = own_head.shape[1]
    return pl.pallas_call(
        logits_kernel,
        in_specs=[
            pl.BlockSpec(memory_space=pltpu.SMEM),
            pl.BlockSpec(memory_space=pl.ANY),
            pl.BlockSpec(memory_space=pl.ANY),
            pl.BlockSpec(memory_space=pl.ANY),
        ],
        out_specs=pl.BlockSpec(memory_space=pltpu.VMEM),
        out_shape=jax.ShapeDtypeStruct((copies, 2, count), jnp.float32),
        scratch_shapes=[
            pltpu.VMEM((slots, chunk, D + EXTRA), jnp.bfloat16),
            pltpu.VMEM((D, vocab), jnp.bfloat16),
            pltpu.VMEM((D, vocab), jnp.bfloat16),
            pltpu.VMEM((2, chunk, 2 * vocab), jnp.float32),
            pltpu.VMEM((count, 128), jnp.float32),
            pltpu.SemaphoreType.DMA((slots,)),
            pltpu.SemaphoreType.DMA((3,)),
        ],
        cost_estimate=pl.CostEstimate(
            flops=2 * count * D * 2 * vocab, bytes_accessed=count * D * 2, transcendentals=0
        ),
        compiler_params=pltpu.CompilerParams(vmem_limit_bytes=54 << 20),
        name="vocabulary_stats",
    )(firsts, rows, own_head, other_head)


def update_kernel(gap_ref, noise_ref, out_ref):
    rows = out_ref.shape[0]
    pairs = noise_ref.shape[1]
    for r in range(0, rows, 16):
        deep = min(16, rows - r)
        total = None
        for p in range(pairs):
            term = gap_ref[p] * noise_ref[0, p, r : r + 16, :].astype(jnp.float32)
            total = term if total is None else total + term
        out_ref[r : r + deep, :] = total[:deep]


def update(gap, noise, rows):
    slabs, pairs, padded, width = noise.shape
    return pl.pallas_call(
        update_kernel,
        grid=(slabs,),
        in_specs=[
            pl.BlockSpec(memory_space=pltpu.SMEM),
            pl.BlockSpec((1, pairs, padded, width), lambda c: (c, 0, 0, 0)),
        ],
        out_specs=pl.BlockSpec((rows, width), lambda c: (0, c)),
        out_shape=jax.ShapeDtypeStruct((rows, slabs * width), jnp.float32),
        cost_estimate=pl.CostEstimate(
            flops=2 * pairs * rows * D, bytes_accessed=2 * pairs * padded * D, transcendentals=0
        ),
        compiler_params=pltpu.CompilerParams(vmem_limit_bytes=44 << 20),
        name="update",
    )(gap, noise)


def scattered_sum(partial, axes):
    pieces = lax.all_to_all(partial, axes, 0, 0)
    total = jnp.sum(pieces.astype(jnp.float32), axis=0)
    share = total.shape[0] // 2
    return jnp.concatenate([total[:share], total[share:]], axis=1)


def joined(stats, axes):
    everyone = lax.all_to_all(stats, axes, 0, 0)
    level = everyone[:, 0]
    top = jnp.max(level, axis=0)
    level = top + jnp.log(jnp.sum(jnp.exp(level - top[None]), axis=0))
    return jnp.stack([level, jnp.sum(everyone[:, 1], axis=0)])


def local(hidden_units, residual, down_weight, norm_gain, head, labels, answer_start, seeds, signs):
    core = lax.axis_index("core")
    pop_at, tp_at = places()
    tp_count = lax.axis_size("z") * 2
    pop_count = seeds.shape[0]
    chip_pairs = pop_count // 2
    tokens = hidden_units.shape[1]
    scored = tokens - SKIP
    share = scored // tp_count
    vocab = head.shape[1]
    noise_scale = 0.25 * FF ** (-0.5)
    swap = [(0, 1), (1, 0)]

    other_head = lax.ppermute(head, "core", swap)

    probe, base = products(seeds, hidden_units[0], down_weight, tp_count)
    base = scattered_sum(base, TP)
    probe, base = lax.optimization_barrier((probe, base))
    probe = scattered_sum(probe, TP)

    token_at = SKIP + tp_at * share
    pair_signs = lax.dynamic_slice_in_dim(signs, pop_at * 2, 2).astype(jnp.float32)
    own_residual = lax.dynamic_slice_in_dim(residual[0], token_at, share, 0).astype(jnp.float32)
    layer = (own_residual + base)[None] + pair_signs[:, None, None] * noise_scale * probe[None]
    mean_square = jnp.mean(layer * layer, axis=2, keepdims=True)
    normed = (layer * lax.rsqrt(mean_square + 1e-06) * norm_gain).astype(jnp.bfloat16)
    own_labels = lax.dynamic_slice_in_dim(labels[0], token_at, share, 0)
    slots = jnp.arange(EXTRA, dtype=jnp.int32)[None, :]
    digits = (own_labels[:, None] >> jnp.clip(16 - 8 * slots, 0, 16)) & 255
    digits = jnp.where(slots < 3, digits, 0).astype(jnp.bfloat16)
    normed = jnp.concatenate([normed, jnp.broadcast_to(digits[None], (2, share, EXTRA))], axis=2)

    out_rows = FF // (pop_count * tp_count)
    later_seeds, normed = lax.optimization_barrier((seeds, normed))
    rows = lax.all_gather(normed.reshape(2 * share, D + EXTRA), SAME_CORE, axis=0, tiled=True)
    noise = regenerate(later_seeds, out_rows)

    own_vocab = (pop_at * tp_count + tp_at) * vocab
    other_vocab = ((pop_at + 1 - 2 * core) * tp_count + tp_at) * vocab
    firsts, noise = lax.optimization_barrier((jnp.stack([own_vocab, other_vocab]), noise))
    stats = joined(vocabulary_stats(rows, head, other_head, firsts, tp_count), TP)
    stats = joined(jnp.broadcast_to(stats[None], (chip_pairs,) + stats.shape), ("y_lo", "x"))
    log_prob = (stats[1] - stats[0]).reshape(tp_count, chip_pairs, 2, share)
    positions = SKIP + jnp.arange(scored, dtype=jnp.int32).reshape(tp_count, 1, share)
    own_starts = lax.dynamic_index_in_dim(answer_start.reshape(chip_pairs, 2), core, 1, keepdims=False)
    mask = (positions >= own_starts[None, :, None]).astype(jnp.float32)
    own_fitness = jnp.sum(log_prob * mask[:, :, None, :], axis=(0, 3)) / (tokens - own_starts).astype(jnp.float32)[:, None]
    other_fitness = lax.ppermute(own_fitness, "core", swap)
    ordered = jnp.where(
        core == 0,
        jnp.stack([own_fitness, other_fitness], axis=1),
        jnp.stack([other_fitness, own_fitness], axis=1),
    )
    fitness = ordered.reshape(2 * pop_count)
    gap = jnp.sum((fitness * signs.astype(jnp.float32)).reshape(pop_count, 2), axis=1)
    return fitness, update(gap, noise, out_rows)


def solution(mesh):
    fine = Mesh(mesh.devices.reshape(2, 4, 2, 4, 2), ("y_lo", "x", "core", "z", "y_hi"))
    pop = ("y_lo", "x", "core")
    return jax.shard_map(
        local,
        mesh=fine,
        in_specs=(
            P(pop, None, TP),
            P(pop, None, None),
            P(TP, None),
            P(),
            P(None, pop + TP),
            P(pop, None),
            P(),
            P(),
            P(),
        ),
        out_specs=(P(), P(pop + TP, None)),
        check_vma=False,
    )
```

```python
import functools

import jax
import jax.numpy as jnp
from jax import lax
from jax.experimental import pallas as pl
from jax.experimental.pallas import tpu as pltpu
from jax.sharding import Mesh, PartitionSpec as P

FF = 18944
D = 3584
SKIP = 32
EXTRA = 128

MUL_A = 739982445
MUL_B = 695872825
SALT = 1013904223
SALT_MIXED = SALT ^ (SALT >> 15)
root_three = 1.7320508075688772

TP = ("z", "y_hi")
SAME_CORE = ("z", "y_hi", "y_lo", "x")


def shifted(hashed, places):
    return lax.shift_right_logical(hashed, jnp.full_like(hashed, places))


def noise_of(index):
    h = index ^ shifted(index, 15)
    h = h * jnp.int32(MUL_A)
    h = h ^ shifted(h, 12)
    h = h * jnp.int32(MUL_B)
    h = h ^ shifted(h, 30) ^ jnp.int32(SALT_MIXED)
    h = h * jnp.int32(MUL_A)
    h = h ^ shifted(h, 12)
    h = h * jnp.int32(MUL_B)
    bits = (h ^ shifted(h, 15)) & jnp.int32(16777215)
    return ((bits.astype(jnp.float32) - 8388607.5) * jnp.float32(root_three / 8388608.0)).astype(jnp.bfloat16)


def places():
    pop_at = (lax.axis_index("y_lo") * lax.axis_size("x") + lax.axis_index("x")) * 2 + lax.axis_index("core")
    return pop_at, lax.axis_index("z") * 2 + lax.axis_index("y_hi")


def probe_step(seeds_ref, hidden_ref, step):
    units = hidden_ref.shape[1]
    half = D // 2
    lane = lax.broadcasted_iota(jnp.int32, (256, 256), 1)
    index = lax.broadcasted_iota(jnp.int32, (256, 256), 0) * D + jnp.where(lane < 128, lane, lane + (half - 128))
    pop_at, tp_at = places()
    at = seeds_ref[pop_at] * jnp.int32(1540483477) + tp_at * jnp.int32(units * D) + step * 128
    total = None
    for k in range(0, units, 256):
        depth = min(256, units - k)
        noise = noise_of(index[:depth] + (at + k * D))
        part = jnp.dot(hidden_ref[SKIP:, k : k + depth], noise, preferred_element_type=jnp.float32)
        total = part if total is None else total + part
    return total[:, :128], total[:, 128:]


def put_shares(ref, cols, left, right):
    share = ref.shape[1] // 2
    for t in range(ref.shape[0]):
        rows = slice(t * share, (t + 1) * share)
        ref[t, :, cols] = jnp.concatenate([left[rows], right[rows]], axis=0).astype(ref.dtype)


def first_kernel(seeds_ref, hidden_ref, weight_hbm, probe_ref, base_ref, weight_ref, sems, *, steps):
    half = D // 2
    wide = half // 2
    copies = []
    for c in range(4):
        cols = slice((c % 2) * half + (c // 2) * wide, (c % 2) * half + (c // 2 + 1) * wide)
        copies.append(pltpu.make_async_copy(weight_hbm.at[:, cols], weight_ref.at[c], sems.at[c]))
        copies[-1].start()
    for step in range(steps):
        put_shares(probe_ref, slice(step * 128, step * 128 + 128), *probe_step(seeds_ref, hidden_ref, step))
    for c in range(0, 4, 2):
        sides = []
        for side in (c, c + 1):
            copies[side].wait()
            sides.append(jnp.dot(hidden_ref[SKIP:, :], weight_ref[side], preferred_element_type=jnp.float32))
        put_shares(base_ref, slice((c // 2) * wide, (c // 2 + 1) * wide), *sides)


def rest_kernel(seeds_ref, hidden_ref, _, probe_ref, *, first_step):
    put_shares(probe_ref, slice(None), *probe_step(seeds_ref, hidden_ref, pl.program_id(0) + first_step))


def products(seeds, hidden, weight, shares, first_steps=2):
    tokens, units = hidden.shape
    share = (tokens - SKIP) // shares
    half = D // 2
    steps = half // 128
    probe_shape = jax.ShapeDtypeStruct((shares, 2 * share, half), jnp.bfloat16)
    base_shape = jax.ShapeDtypeStruct((shares, 2 * share, half), jnp.float32)
    scalar = pl.BlockSpec(memory_space=pltpu.SMEM)
    whole = pl.BlockSpec((tokens, units), lambda i: (0, 0))
    params = pltpu.CompilerParams(vmem_limit_bytes=44 << 20)

    def cost(count):
        return pl.CostEstimate(flops=units * count * 256 * 2000, bytes_accessed=units * count * 256, transcendentals=0)

    probe, base = pl.pallas_call(
        functools.partial(first_kernel, steps=first_steps),
        grid=(1,),
        in_specs=[scalar, whole, pl.BlockSpec(memory_space=pl.ANY)],
        out_specs=[
            pl.BlockSpec((shares, 2 * share, first_steps * 128), lambda i: (0, 0, 0)),
            pl.BlockSpec((shares, 2 * share, half), lambda i: (0, 0, 0)),
        ],
        out_shape=[probe_shape, base_shape],
        scratch_shapes=[pltpu.VMEM((4, units, half // 2), jnp.bfloat16), pltpu.SemaphoreType.DMA((4,))],
        cost_estimate=cost(first_steps),
        compiler_params=params,
        name="base_and_probe",
    )(seeds, hidden, weight)
    probe = pl.pallas_call(
        functools.partial(rest_kernel, first_step=first_steps),
        grid=(steps - first_steps,),
        in_specs=[scalar, whole, pl.BlockSpec(memory_space=pl.ANY)],
        out_specs=pl.BlockSpec((shares, 2 * share, 128), lambda i: (0, 0, i + first_steps)),
        out_shape=probe_shape,
        input_output_aliases={2: 0},
        cost_estimate=cost(steps - first_steps),
        compiler_params=params,
        name="probe",
    )(seeds, hidden, probe)
    return probe, base


def regenerate_kernel(seeds_ref, out_ref, *, out_rows):
    slabs, depth, width = out_ref.shape
    pairs = seeds_ref.shape[0]
    pop_at, tp_at = places()
    first = (pop_at * lax.axis_size("z") * 2 + tp_at) * out_rows + pl.program_id(0) * (depth // pairs)
    index = seeds_ref[...] * jnp.int32(1540483477) + lax.broadcasted_iota(jnp.int32, (pairs, width), 1)
    for r in range(depth // pairs):
        for c in range(slabs):
            out_ref[c, r * pairs : (r + 1) * pairs, :] = noise_of(index + ((first + r) * D + c * width))


def regenerate(seeds, rows, width=512, rows_each=4):
    pairs = seeds.shape[0]
    return pl.pallas_call(
        functools.partial(regenerate_kernel, out_rows=rows),
        grid=(rows // rows_each,),
        in_specs=[pl.BlockSpec((pairs, 1), lambda i: (0, 0))],
        out_specs=pl.BlockSpec((D // width, rows_each * pairs, width), lambda i: (0, i, 0)),
        out_shape=jax.ShapeDtypeStruct((D // width, rows * pairs, width), jnp.bfloat16),
        cost_estimate=pl.CostEstimate(
            flops=pairs * rows * D * 2000, bytes_accessed=pairs * rows * D * 2, transcendentals=0
        ),
        compiler_params=pltpu.CompilerParams(vmem_limit_bytes=50 << 20),
        name="regenerate",
    )(seeds.reshape(pairs, 1))


def logits_kernel(
    first_ref, rows_hbm, own_hbm, other_hbm, out_ref, rows_ref, own_ref, other_ref, held_ref, stats_ref, sems, head_sems
):
    slots, chunk, _ = rows_ref.shape
    chunks = rows_hbm.shape[0] // chunk
    vocab = own_ref.shape[1]
    lanes = lax.broadcasted_iota(jnp.int32, (1, 128), 1).astype(jnp.float32)

    def fetch(i):
        return pltpu.make_async_copy(
            rows_hbm.at[pl.ds(i * chunk, chunk), :], rows_ref.at[i % slots], sems.at[i % slots]
        )

    early = vocab // 3
    heads = [
        pltpu.make_async_copy(own_hbm.at[:, :early], own_ref.at[:, :early], head_sems.at[0]),
        pltpu.make_async_copy(own_hbm.at[:, early:], own_ref.at[:, early:], head_sems.at[1]),
        pltpu.make_async_copy(other_hbm, other_ref, head_sems.at[2]),
    ]

    def multiply(i):
        rows = rows_ref[i % slots, :, :D]
        if i == 0:
            for copy, ref, cols, at in (
                (heads[0], own_ref, slice(0, early), 0),
                (heads[1], own_ref, slice(early, vocab), early),
                (heads[2], other_ref, slice(0, vocab), vocab),
            ):
                copy.wait()
                made = jnp.dot(rows, ref[:, cols], preferred_element_type=jnp.float32)
                held_ref[0, :, at : at + made.shape[1]] = made
        else:
            held_ref[i % 2, :, :vocab] = jnp.dot(rows, own_ref[...], preferred_element_type=jnp.float32)
            held_ref[i % 2, :, vocab:] = jnp.dot(rows, other_ref[...], preferred_element_type=jnp.float32)

    def absorb(i):
        slot = i % 2
        high = held_ref[slot, :, :128]
        for c in range(128, 2 * vocab, 128):
            high = jnp.maximum(high, held_ref[slot, :, c : c + 128])
        high = jnp.broadcast_to(jnp.max(high, axis=1, keepdims=True), (chunk, 128))
        digits = rows_ref[i % slots, :, D : D + EXTRA].astype(jnp.float32)
        label = digits[:, 0:1] * 65536.0 + digits[:, 1:2] * 256.0 + digits[:, 2:3]
        label = [jnp.broadcast_to(label - first_ref[h].astype(jnp.float32), (chunk, 128)) for h in range(2)]
        total = jnp.zeros((chunk, 128), jnp.float32)
        hit = jnp.zeros((chunk, 128), jnp.float32)
        for c in range(0, 2 * vocab, 128):
            slab = held_ref[slot, :, c : c + 128]
            total = total + jnp.exp(slab - high)
            hit = jnp.where(lanes + float(c % vocab) == label[c // vocab], slab, hit)
        total = jnp.sum(total, axis=1, keepdims=True)
        hit = jnp.sum(hit, axis=1, keepdims=True)
        lane = lax.broadcasted_iota(jnp.int32, (chunk, 128), 1)
        stats_ref[i * chunk : (i + 1) * chunk, :] = jnp.where(lane == 0, high + jnp.log(total), hit)

    fetch(0).start()
    for copy in heads:
        copy.start()
    for i in range(1, min(slots - 1, chunks)):
        fetch(i).start()
    for i in range(chunks):
        fetch(i).wait()
        multiply(i)
        if i:
            absorb(i - 1)
        if i + slots - 1 < chunks:
            fetch(i + slots - 1).start()
    absorb(chunks - 1)
    both = stats_ref[...].T[:2, :]
    for t in range(out_ref.shape[0]):
        out_ref[t] = both


def vocabulary_stats(rows, own_head, other_head, firsts, copies, chunk=256, slots=4):
    count = rows.shape[0]
    vocab = own_head.shape[1]
    return pl.pallas_call(
        logits_kernel,
        in_specs=[
            pl.BlockSpec(memory_space=pltpu.SMEM),
            pl.BlockSpec(memory_space=pl.ANY),
            pl.BlockSpec(memory_space=pl.ANY),
            pl.BlockSpec(memory_space=pl.ANY),
        ],
        out_specs=pl.BlockSpec(memory_space=pltpu.VMEM),
        out_shape=jax.ShapeDtypeStruct((copies, 2, count), jnp.float32),
        scratch_shapes=[
            pltpu.VMEM((slots, chunk, D + EXTRA), jnp.bfloat16),
            pltpu.VMEM((D, vocab), jnp.bfloat16),
            pltpu.VMEM((D, vocab), jnp.bfloat16),
            pltpu.VMEM((2, chunk, 2 * vocab), jnp.float32),
            pltpu.VMEM((count, 128), jnp.float32),
            pltpu.SemaphoreType.DMA((slots,)),
            pltpu.SemaphoreType.DMA((3,)),
        ],
        cost_estimate=pl.CostEstimate(
            flops=2 * count * D * 2 * vocab, bytes_accessed=count * D * 2, transcendentals=0
        ),
        compiler_params=pltpu.CompilerParams(vmem_limit_bytes=54 << 20),
        name="vocabulary_stats",
    )(firsts, rows, own_head, other_head)


def update_kernel(gap_ref, noise_ref, out_ref, *, pairs):
    rows = out_ref.shape[0]
    gap = gap_ref[...]
    high = gap.astype(jnp.bfloat16).astype(jnp.float32)
    middle = (gap - high).astype(jnp.bfloat16).astype(jnp.float32)
    low = gap - high - middle
    at = (16, 16 * pairs)
    own = lax.broadcasted_iota(jnp.int32, at, 0) * pairs
    lane = lax.broadcasted_iota(jnp.int32, at, 1)
    mine = (lane >= own) & (lane < own + pairs)
    left = jnp.concatenate([jnp.where(mine, jnp.broadcast_to(part, at), 0.0) for part in (high, middle, low)], axis=0)
    left = left.astype(jnp.bfloat16)
    for r in range(0, rows, 16):
        deep = min(16, rows - r)
        parts = jnp.dot(
            left[:, : deep * pairs],
            noise_ref[0, r * pairs : (r + deep) * pairs, :],
            preferred_element_type=jnp.float32,
        )
        total = parts[:16] + parts[16:32] + parts[32:]
        out_ref[r : r + deep, :] = total[:deep]


def update(gap, noise, rows):
    slabs, depth, width = noise.shape
    pairs = gap.shape[0]
    return pl.pallas_call(
        functools.partial(update_kernel, pairs=pairs),
        grid=(slabs,),
        in_specs=[
            pl.BlockSpec((1, 16 * pairs), lambda c: (0, 0)),
            pl.BlockSpec((1, depth, width), lambda c: (c, 0, 0)),
        ],
        out_specs=pl.BlockSpec((rows, width), lambda c: (0, c)),
        out_shape=jax.ShapeDtypeStruct((rows, slabs * width), jnp.float32),
        cost_estimate=pl.CostEstimate(flops=2 * depth * D, bytes_accessed=2 * depth * D, transcendentals=0),
        compiler_params=pltpu.CompilerParams(vmem_limit_bytes=44 << 20),
        name="update",
    )(jnp.tile(gap, 16).reshape(1, 16 * pairs), noise)


def scattered_sum(partial, axes):
    pieces = lax.all_to_all(partial, axes, 0, 0)
    total = jnp.sum(pieces.astype(jnp.float32), axis=0)
    share = total.shape[0] // 2
    return jnp.concatenate([total[:share], total[share:]], axis=1)


def joined(stats, axes):
    everyone = lax.all_to_all(stats, axes, 0, 0)
    level = everyone[:, 0]
    top = jnp.max(level, axis=0)
    level = top + jnp.log(jnp.sum(jnp.exp(level - top[None]), axis=0))
    return jnp.stack([level, jnp.sum(everyone[:, 1], axis=0)])


def local(hidden_units, residual, down_weight, norm_gain, head, labels, answer_start, seeds, signs):
    core = lax.axis_index("core")
    pop_at, tp_at = places()
    tp_count = lax.axis_size("z") * 2
    pop_count = seeds.shape[0]
    chip_pairs = pop_count // 2
    tokens = hidden_units.shape[1]
    scored = tokens - SKIP
    share = scored // tp_count
    vocab = head.shape[1]
    noise_scale = 0.25 * FF ** (-0.5)
    swap = [(0, 1), (1, 0)]

    other_head = lax.ppermute(head, "core", swap)

    probe, base = products(seeds, hidden_units[0], down_weight, tp_count)
    base = scattered_sum(base, TP)
    probe, base = lax.optimization_barrier((probe, base))
    probe = scattered_sum(probe, TP)

    token_at = SKIP + tp_at * share
    pair_signs = lax.dynamic_slice_in_dim(signs, pop_at * 2, 2).astype(jnp.float32)
    own_residual = lax.dynamic_slice_in_dim(residual[0], token_at, share, 0).astype(jnp.float32)
    layer = (own_residual + base)[None] + pair_signs[:, None, None] * noise_scale * probe[None]
    mean_square = jnp.mean(layer * layer, axis=2, keepdims=True)
    normed = (layer * lax.rsqrt(mean_square + 1e-06) * norm_gain).astype(jnp.bfloat16)
    own_labels = lax.dynamic_slice_in_dim(labels[0], token_at, share, 0)
    slots = jnp.arange(EXTRA, dtype=jnp.int32)[None, :]
    digits = (own_labels[:, None] >> jnp.clip(16 - 8 * slots, 0, 16)) & 255
    digits = jnp.where(slots < 3, digits, 0).astype(jnp.bfloat16)
    normed = jnp.concatenate([normed, jnp.broadcast_to(digits[None], (2, share, EXTRA))], axis=2)

    out_rows = FF // (pop_count * tp_count)
    later_seeds, normed = lax.optimization_barrier((seeds, normed))
    rows = lax.all_gather(normed.reshape(2 * share, D + EXTRA), SAME_CORE, axis=0, tiled=True)
    noise = regenerate(later_seeds, out_rows)

    own_vocab = (pop_at * tp_count + tp_at) * vocab
    other_vocab = ((pop_at + 1 - 2 * core) * tp_count + tp_at) * vocab
    firsts, noise = lax.optimization_barrier((jnp.stack([own_vocab, other_vocab]), noise))
    stats = joined(vocabulary_stats(rows, head, other_head, firsts, tp_count), TP)
    stats = joined(jnp.broadcast_to(stats[None], (chip_pairs,) + stats.shape), ("y_lo", "x"))
    log_prob = (stats[1] - stats[0]).reshape(tp_count, chip_pairs, 2, share)
    positions = SKIP + jnp.arange(scored, dtype=jnp.int32).reshape(tp_count, 1, share)
    own_starts = lax.dynamic_index_in_dim(answer_start.reshape(chip_pairs, 2), core, 1, keepdims=False)
    mask = (positions >= own_starts[None, :, None]).astype(jnp.float32)
    own_fitness = jnp.sum(log_prob * mask[:, :, None, :], axis=(0, 3)) / (tokens - own_starts).astype(jnp.float32)[:, None]
    other_fitness = lax.ppermute(own_fitness, "core", swap)
    ordered = jnp.where(
        core == 0,
        jnp.stack([own_fitness, other_fitness], axis=1),
        jnp.stack([other_fitness, own_fitness], axis=1),
    )
    fitness = ordered.reshape(2 * pop_count)
    gap = jnp.sum((fitness * signs.astype(jnp.float32)).reshape(pop_count, 2), axis=1)
    return fitness, update(gap, noise, out_rows)


def solution(mesh):
    fine = Mesh(mesh.devices.reshape(2, 4, 2, 4, 2), ("y_lo", "x", "core", "z", "y_hi"))
    pop = ("y_lo", "x", "core")
    return jax.shard_map(
        local,
        mesh=fine,
        in_specs=(
            P(pop, None, TP),
            P(pop, None, None),
            P(TP, None),
            P(),
            P(None, pop + TP),
            P(pop, None),
            P(),
            P(),
            P(),
        ),
        out_specs=(P(), P(pop + TP, None)),
        check_vma=False,
    )
```

```python
import functools

import jax
import jax.numpy as jnp
from jax import lax
from jax.experimental import pallas as pl
from jax.experimental.pallas import tpu as pltpu
from jax.sharding import Mesh, PartitionSpec as P

FF = 18944
D = 3584
SKIP = 32
EXTRA = 128

MUL_A = 739982445
MUL_B = 695872825
SALT = 1013904223
SALT_MIXED = SALT ^ (SALT >> 15)
root_three = 1.7320508075688772

TP = ("z", "y_hi")
SAME_CORE = ("z", "y_hi", "y_lo", "x")


def shifted(hashed, places):
    return lax.shift_right_logical(hashed, jnp.full_like(hashed, places))


def noise_of(index):
    h = index ^ shifted(index, 15)
    h = h * jnp.int32(MUL_A)
    h = h ^ shifted(h, 12)
    h = h * jnp.int32(MUL_B)
    h = h ^ shifted(h, 30) ^ jnp.int32(SALT_MIXED)
    h = h * jnp.int32(MUL_A)
    h = h ^ shifted(h, 12)
    h = h * jnp.int32(MUL_B)
    bits = (h ^ shifted(h, 15)) & jnp.int32(16777215)
    return ((bits.astype(jnp.float32) - 8388607.5) * jnp.float32(root_three / 8388608.0)).astype(jnp.bfloat16)


def places():
    pop_at = (lax.axis_index("y_lo") * lax.axis_size("x") + lax.axis_index("x")) * 2 + lax.axis_index("core")
    return pop_at, lax.axis_index("z") * 2 + lax.axis_index("y_hi")


def probe_step(seeds_ref, hidden_ref, step):
    units = hidden_ref.shape[1]
    half = D // 2
    lane = lax.broadcasted_iota(jnp.int32, (256, 256), 1)
    index = lax.broadcasted_iota(jnp.int32, (256, 256), 0) * D + jnp.where(lane < 128, lane, lane + (half - 128))
    pop_at, tp_at = places()
    at = seeds_ref[pop_at] * jnp.int32(1540483477) + tp_at * jnp.int32(units * D) + step * 128
    total = None
    for k in range(0, units, 256):
        depth = min(256, units - k)
        noise = noise_of(index[:depth] + (at + k * D))
        part = jnp.dot(hidden_ref[SKIP:, k : k + depth], noise, preferred_element_type=jnp.float32)
        total = part if total is None else total + part
    return total[:, :128], total[:, 128:]


def put_shares(ref, cols, left, right):
    share = ref.shape[1] // 2
    for t in range(ref.shape[0]):
        rows = slice(t * share, (t + 1) * share)
        ref[t, :, cols] = jnp.concatenate([left[rows], right[rows]], axis=0).astype(ref.dtype)


def first_kernel(seeds_ref, hidden_ref, weight_hbm, probe_ref, base_ref, weight_ref, sems, *, steps):
    half = D // 2
    wide = half // 2
    copies = []
    for c in range(4):
        cols = slice((c % 2) * half + (c // 2) * wide, (c % 2) * half + (c // 2 + 1) * wide)
        copies.append(pltpu.make_async_copy(weight_hbm.at[:, cols], weight_ref.at[c], sems.at[c]))
        copies[-1].start()
    for step in range(steps):
        put_shares(probe_ref, slice(step * 128, step * 128 + 128), *probe_step(seeds_ref, hidden_ref, step))
    for c in range(0, 4, 2):
        sides = []
        for side in (c, c + 1):
            copies[side].wait()
            sides.append(jnp.dot(hidden_ref[SKIP:, :], weight_ref[side], preferred_element_type=jnp.float32))
        put_shares(base_ref, slice((c // 2) * wide, (c // 2 + 1) * wide), *sides)


def rest_kernel(seeds_ref, hidden_ref, _, probe_ref, *, first_step):
    put_shares(probe_ref, slice(None), *probe_step(seeds_ref, hidden_ref, pl.program_id(0) + first_step))


def products(seeds, hidden, weight, shares, first_steps=2):
    tokens, units = hidden.shape
    share = (tokens - SKIP) // shares
    half = D // 2
    steps = half // 128
    probe_shape = jax.ShapeDtypeStruct((shares, 2 * share, half), jnp.bfloat16)
    base_shape = jax.ShapeDtypeStruct((shares, 2 * share, half), jnp.float32)
    scalar = pl.BlockSpec(memory_space=pltpu.SMEM)
    whole = pl.BlockSpec((tokens, units), lambda i: (0, 0))
    params = pltpu.CompilerParams(vmem_limit_bytes=44 << 20)

    def cost(count):
        return pl.CostEstimate(flops=units * count * 256 * 2000, bytes_accessed=units * count * 256, transcendentals=0)

    probe, base = pl.pallas_call(
        functools.partial(first_kernel, steps=first_steps),
        grid=(1,),
        in_specs=[scalar, whole, pl.BlockSpec(memory_space=pl.ANY)],
        out_specs=[
            pl.BlockSpec((shares, 2 * share, first_steps * 128), lambda i: (0, 0, 0)),
            pl.BlockSpec((shares, 2 * share, half), lambda i: (0, 0, 0)),
        ],
        out_shape=[probe_shape, base_shape],
        scratch_shapes=[pltpu.VMEM((4, units, half // 2), jnp.bfloat16), pltpu.SemaphoreType.DMA((4,))],
        cost_estimate=cost(first_steps),
        compiler_params=params,
        name="base_and_probe",
    )(seeds, hidden, weight)
    probe = pl.pallas_call(
        functools.partial(rest_kernel, first_step=first_steps),
        grid=(steps - first_steps,),
        in_specs=[scalar, whole, pl.BlockSpec(memory_space=pl.ANY)],
        out_specs=pl.BlockSpec((shares, 2 * share, 128), lambda i: (0, 0, i + first_steps)),
        out_shape=probe_shape,
        input_output_aliases={2: 0},
        cost_estimate=cost(steps - first_steps),
        compiler_params=params,
        name="probe",
    )(seeds, hidden, probe)
    return probe, base


def regenerate_kernel(seeds_ref, out_ref, *, out_rows):
    slabs, depth, width = out_ref.shape
    pairs = seeds_ref.shape[0]
    pop_at, tp_at = places()
    first = (pop_at * lax.axis_size("z") * 2 + tp_at) * out_rows + pl.program_id(0) * (depth // pairs)
    index = seeds_ref[...] * jnp.int32(1540483477) + lax.broadcasted_iota(jnp.int32, (pairs, width), 1)
    for r in range(depth // pairs):
        for c in range(slabs):
            out_ref[c, r * pairs : (r + 1) * pairs, :] = noise_of(index + ((first + r) * D + c * width))


def regenerate(seeds, rows, width=512, rows_each=4):
    pairs = seeds.shape[0]
    return pl.pallas_call(
        functools.partial(regenerate_kernel, out_rows=rows),
        grid=(rows // rows_each,),
        in_specs=[pl.BlockSpec((pairs, 1), lambda i: (0, 0))],
        out_specs=pl.BlockSpec((D // width, rows_each * pairs, width), lambda i: (0, i, 0)),
        out_shape=jax.ShapeDtypeStruct((D // width, rows * pairs, width), jnp.bfloat16),
        cost_estimate=pl.CostEstimate(
            flops=pairs * rows * D * 2000, bytes_accessed=pairs * rows * D * 2, transcendentals=0
        ),
        compiler_params=pltpu.CompilerParams(vmem_limit_bytes=50 << 20),
        name="regenerate",
    )(seeds.reshape(pairs, 1))


def logits_kernel(
    first_ref, rows_hbm, own_hbm, other_hbm, out_ref, rows_ref, heads_ref, held_ref, stats_ref, sems, head_sems
):
    slots, chunk, _ = rows_ref.shape
    chunks = rows_hbm.shape[0] // chunk
    vocab = own_hbm.shape[1]
    lanes = lax.broadcasted_iota(jnp.int32, (1, 128), 1).astype(jnp.float32)

    def fetch(i):
        return pltpu.make_async_copy(
            rows_hbm.at[pl.ds(i * chunk, chunk), :], rows_ref.at[i % slots], sems.at[i % slots]
        )

    third = vocab // 3
    pieces = []
    for hbm, at, cuts in ((own_hbm, 0, (0, 2 * third, vocab)), (other_hbm, vocab, (0, third, vocab))):
        for first, last in zip(cuts[:-1], cuts[1:]):
            to = heads_ref.at[:, at + first : at + last]
            pieces.append(pltpu.make_async_copy(hbm.at[:, first:last], to, head_sems.at[len(pieces)]))

    def multiply(i):
        rows = rows_ref[i % slots, :, :D]
        if i == 0:
            for part, waits in enumerate((pieces[:1], pieces[1:3], pieces[3:])):
                for piece in waits:
                    piece.wait()
                cols = slice(2 * part * third, 2 * (part + 1) * third)
                held_ref[0, :, cols] = jnp.dot(rows, heads_ref[:, cols], preferred_element_type=jnp.float32)
        else:
            held_ref[i % 2] = jnp.dot(rows, heads_ref[...], preferred_element_type=jnp.float32)

    def absorb(i):
        slot = i % 2
        high = held_ref[slot, :, :128]
        for c in range(128, 2 * vocab, 128):
            high = jnp.maximum(high, held_ref[slot, :, c : c + 128])
        high = jnp.broadcast_to(jnp.max(high, axis=1, keepdims=True), (chunk, 128))
        digits = rows_ref[i % slots, :, D : D + EXTRA].astype(jnp.float32)
        label = digits[:, 0:1] * 65536.0 + digits[:, 1:2] * 256.0 + digits[:, 2:3]
        label = [jnp.broadcast_to(label - first_ref[h].astype(jnp.float32), (chunk, 128)) for h in range(2)]
        total = jnp.zeros((chunk, 128), jnp.float32)
        hit = jnp.zeros((chunk, 128), jnp.float32)
        for c in range(0, 2 * vocab, 128):
            slab = held_ref[slot, :, c : c + 128]
            total = total + jnp.exp(slab - high)
            hit = jnp.where(lanes + float(c % vocab) == label[c // vocab], slab, hit)
        total = jnp.sum(total, axis=1, keepdims=True)
        hit = jnp.sum(hit, axis=1, keepdims=True)
        lane = lax.broadcasted_iota(jnp.int32, (chunk, 128), 1)
        stats_ref[i * chunk : (i + 1) * chunk, :] = jnp.where(lane == 0, high + jnp.log(total), hit)

    fetch(0).start()
    for piece in pieces:
        piece.start()
    for i in range(1, min(slots - 1, chunks)):
        fetch(i).start()
    for i in range(chunks):
        fetch(i).wait()
        multiply(i)
        if i:
            absorb(i - 1)
        if i + slots - 1 < chunks:
            fetch(i + slots - 1).start()
    absorb(chunks - 1)
    both = stats_ref[...].T[:2, :]
    for t in range(out_ref.shape[0]):
        out_ref[t] = both


def vocabulary_stats(rows, own_head, other_head, firsts, copies, chunk=256, slots=4):
    count = rows.shape[0]
    vocab = own_head.shape[1]
    return pl.pallas_call(
        logits_kernel,
        in_specs=[
            pl.BlockSpec(memory_space=pltpu.SMEM),
            pl.BlockSpec(memory_space=pl.ANY),
            pl.BlockSpec(memory_space=pl.ANY),
            pl.BlockSpec(memory_space=pl.ANY),
        ],
        out_specs=pl.BlockSpec(memory_space=pltpu.VMEM),
        out_shape=jax.ShapeDtypeStruct((copies, 2, count), jnp.float32),
        scratch_shapes=[
            pltpu.VMEM((slots, chunk, D + EXTRA), jnp.bfloat16),
            pltpu.VMEM((D, 2 * vocab), jnp.bfloat16),
            pltpu.VMEM((2, chunk, 2 * vocab), jnp.float32),
            pltpu.VMEM((count, 128), jnp.float32),
            pltpu.SemaphoreType.DMA((slots,)),
            pltpu.SemaphoreType.DMA((4,)),
        ],
        cost_estimate=pl.CostEstimate(
            flops=2 * count * D * 2 * vocab, bytes_accessed=count * D * 2, transcendentals=0
        ),
        compiler_params=pltpu.CompilerParams(vmem_limit_bytes=54 << 20),
        name="vocabulary_stats",
    )(firsts, rows, own_head, other_head)


def update_kernel(gap_ref, noise_hbm, out_hbm, noise_ref, out_ref, in_sems, out_sems, *, pairs):
    slabs, _, width = noise_ref.shape
    rows = out_ref.shape[1]
    reads = [pltpu.make_async_copy(noise_hbm.at[c], noise_ref.at[c], in_sems.at[c]) for c in range(slabs)]
    writes = [
        pltpu.make_async_copy(out_ref.at[c], out_hbm.at[:, c * width : (c + 1) * width], out_sems.at[c])
        for c in range(slabs)
    ]
    for read in reads:
        read.start()
    gap = gap_ref[...]
    high = gap.astype(jnp.bfloat16).astype(jnp.float32)
    middle = (gap - high).astype(jnp.bfloat16).astype(jnp.float32)
    low = gap - high - middle
    at = (16, 16 * pairs)
    own = lax.broadcasted_iota(jnp.int32, at, 0) * pairs
    lane = lax.broadcasted_iota(jnp.int32, at, 1)
    mine = (lane >= own) & (lane < own + pairs)
    left = jnp.concatenate([jnp.where(mine, jnp.broadcast_to(part, at), 0.0) for part in (high, middle, low)], axis=0)
    left = left.astype(jnp.bfloat16)
    for c in range(slabs):
        reads[c].wait()
        for r in range(0, rows, 16):
            deep = min(16, rows - r)
            parts = jnp.dot(
                left[:, : deep * pairs],
                noise_ref[c, r * pairs : (r + deep) * pairs, :],
                preferred_element_type=jnp.float32,
            )
            total = parts[:16] + parts[16:32] + parts[32:]
            out_ref[c, r : r + deep, :] = total[:deep]
        writes[c].start()
    for write in writes:
        write.wait()


def update(gap, noise, rows):
    slabs, depth, width = noise.shape
    pairs = gap.shape[0]
    return pl.pallas_call(
        functools.partial(update_kernel, pairs=pairs),
        in_specs=[pl.BlockSpec(memory_space=pltpu.VMEM), pl.BlockSpec(memory_space=pl.ANY)],
        out_specs=pl.BlockSpec(memory_space=pl.ANY),
        out_shape=jax.ShapeDtypeStruct((rows, slabs * width), jnp.float32),
        scratch_shapes=[
            pltpu.VMEM((slabs, depth, width), jnp.bfloat16),
            pltpu.VMEM((slabs, rows, width), jnp.float32),
            pltpu.SemaphoreType.DMA((slabs,)),
            pltpu.SemaphoreType.DMA((slabs,)),
        ],
        cost_estimate=pl.CostEstimate(flops=2 * depth * D, bytes_accessed=2 * depth * D, transcendentals=0),
        compiler_params=pltpu.CompilerParams(vmem_limit_bytes=50 << 20),
        name="update",
    )(jnp.tile(gap, 16).reshape(1, 16 * pairs), noise)


def scattered_sum(partial, axes):
    pieces = lax.all_to_all(partial, axes, 0, 0)
    total = jnp.sum(pieces.astype(jnp.float32), axis=0)
    share = total.shape[0] // 2
    return jnp.concatenate([total[:share], total[share:]], axis=1)


def joined(stats, axes):
    everyone = lax.all_to_all(stats, axes, 0, 0)
    level = everyone[:, 0]
    top = jnp.max(level, axis=0)
    level = top + jnp.log(jnp.sum(jnp.exp(level - top[None]), axis=0))
    return jnp.stack([level, jnp.sum(everyone[:, 1], axis=0)])


def local(hidden_units, residual, down_weight, norm_gain, head, labels, answer_start, seeds, signs):
    core = lax.axis_index("core")
    pop_at, tp_at = places()
    tp_count = lax.axis_size("z") * 2
    pop_count = seeds.shape[0]
    chip_pairs = pop_count // 2
    tokens = hidden_units.shape[1]
    scored = tokens - SKIP
    share = scored // tp_count
    vocab = head.shape[1]
    noise_scale = 0.25 * FF ** (-0.5)
    swap = [(0, 1), (1, 0)]

    other_head = lax.ppermute(head, "core", swap)

    probe, base = products(seeds, hidden_units[0], down_weight, tp_count)
    base = scattered_sum(base, TP)
    probe, base = lax.optimization_barrier((probe, base))
    probe = scattered_sum(probe, TP)

    token_at = SKIP + tp_at * share
    pair_signs = lax.dynamic_slice_in_dim(signs, pop_at * 2, 2).astype(jnp.float32)
    own_residual = lax.dynamic_slice_in_dim(residual[0], token_at, share, 0).astype(jnp.float32)
    layer = (own_residual + base)[None] + pair_signs[:, None, None] * noise_scale * probe[None]
    mean_square = jnp.mean(layer * layer, axis=2, keepdims=True)
    normed = (layer * lax.rsqrt(mean_square + 1e-06) * norm_gain).astype(jnp.bfloat16)
    own_labels = lax.dynamic_slice_in_dim(labels[0], token_at, share, 0)
    slots = jnp.arange(EXTRA, dtype=jnp.int32)[None, :]
    digits = (own_labels[:, None] >> jnp.clip(16 - 8 * slots, 0, 16)) & 255
    digits = jnp.where(slots < 3, digits, 0).astype(jnp.bfloat16)
    normed = jnp.concatenate([normed, jnp.broadcast_to(digits[None], (2, share, EXTRA))], axis=2)

    out_rows = FF // (pop_count * tp_count)
    later_seeds, normed = lax.optimization_barrier((seeds, normed))
    rows = lax.all_gather(normed.reshape(2 * share, D + EXTRA), SAME_CORE, axis=0, tiled=True)
    noise = regenerate(later_seeds, out_rows)

    own_vocab = (pop_at * tp_count + tp_at) * vocab
    other_vocab = ((pop_at + 1 - 2 * core) * tp_count + tp_at) * vocab
    firsts, noise = lax.optimization_barrier((jnp.stack([own_vocab, other_vocab]), noise))
    stats = joined(vocabulary_stats(rows, head, other_head, firsts, tp_count), TP)
    stats = joined(jnp.broadcast_to(stats[None], (chip_pairs,) + stats.shape), ("y_lo", "x"))
    log_prob = (stats[1] - stats[0]).reshape(tp_count, chip_pairs, 2, share)
    positions = SKIP + jnp.arange(scored, dtype=jnp.int32).reshape(tp_count, 1, share)
    own_starts = lax.dynamic_index_in_dim(answer_start.reshape(chip_pairs, 2), core, 1, keepdims=False)
    mask = (positions >= own_starts[None, :, None]).astype(jnp.float32)
    own_fitness = jnp.sum(log_prob * mask[:, :, None, :], axis=(0, 3)) / (tokens - own_starts).astype(jnp.float32)[:, None]
    other_fitness = lax.ppermute(own_fitness, "core", swap)
    ordered = jnp.where(
        core == 0,
        jnp.stack([own_fitness, other_fitness], axis=1),
        jnp.stack([other_fitness, own_fitness], axis=1),
    )
    fitness = ordered.reshape(2 * pop_count)
    gap = jnp.sum((fitness * signs.astype(jnp.float32)).reshape(pop_count, 2), axis=1)
    return fitness, update(gap, noise, out_rows)


def solution(mesh):
    fine = Mesh(mesh.devices.reshape(2, 4, 2, 4, 2), ("y_lo", "x", "core", "z", "y_hi"))
    pop = ("y_lo", "x", "core")
    return jax.shard_map(
        local,
        mesh=fine,
        in_specs=(
            P(pop, None, TP),
            P(pop, None, None),
            P(TP, None),
            P(),
            P(None, pop + TP),
            P(pop, None),
            P(),
            P(),
            P(),
        ),
        out_specs=(P(), P(pop + TP, None)),
        check_vma=False,
    )
```

```python
import functools

import jax
import jax.numpy as jnp
from jax import lax
from jax.experimental import pallas as pl
from jax.experimental.pallas import tpu as pltpu
from jax.sharding import Mesh, PartitionSpec as P

FF = 18944
D = 3584
SKIP = 32
EXTRA = 128

MUL_A = 739982445
MUL_B = 695872825
SALT = 1013904223
SALT_MIXED = SALT ^ (SALT >> 15)
root_three = 1.7320508075688772

TP = ("z", "y_hi")
SAME_CORE = ("z", "y_hi", "y_lo", "x")


def shifted(hashed, places):
    return lax.shift_right_logical(hashed, jnp.full_like(hashed, places))


def noise_of(index):
    h = index ^ shifted(index, 15)
    h = h * jnp.int32(MUL_A)
    h = h ^ shifted(h, 12)
    h = h * jnp.int32(MUL_B)
    h = h ^ shifted(h, 30) ^ jnp.int32(SALT_MIXED)
    h = h * jnp.int32(MUL_A)
    h = h ^ shifted(h, 12)
    h = h * jnp.int32(MUL_B)
    bits = (h ^ shifted(h, 15)) & jnp.int32(16777215)
    return ((bits.astype(jnp.float32) - 8388607.5) * jnp.float32(root_three / 8388608.0)).astype(jnp.bfloat16)


def places():
    pop_at = (lax.axis_index("y_lo") * lax.axis_size("x") + lax.axis_index("x")) * 2 + lax.axis_index("core")
    return pop_at, lax.axis_index("z") * 2 + lax.axis_index("y_hi")


def probe_step(seeds_ref, hidden_ref, step):
    units = hidden_ref.shape[1]
    half = D // 2
    lane = lax.broadcasted_iota(jnp.int32, (256, 256), 1)
    index = lax.broadcasted_iota(jnp.int32, (256, 256), 0) * D + jnp.where(lane < 128, lane, lane + (half - 128))
    pop_at, tp_at = places()
    at = seeds_ref[pop_at] * jnp.int32(1540483477) + tp_at * jnp.int32(units * D) + step * 128
    total = None
    for k in range(0, units, 256):
        depth = min(256, units - k)
        noise = noise_of(index[:depth] + (at + k * D))
        part = jnp.dot(hidden_ref[SKIP:, k : k + depth], noise, preferred_element_type=jnp.float32)
        total = part if total is None else total + part
    return total[:, :128], total[:, 128:]


def put_shares(ref, cols, left, right):
    share = ref.shape[1] // 2
    for t in range(ref.shape[0]):
        rows = slice(t * share, (t + 1) * share)
        ref[t, :, cols] = jnp.concatenate([left[rows], right[rows]], axis=0).astype(ref.dtype)


def first_kernel(seeds_ref, hidden_ref, weight_hbm, probe_ref, base_ref, weight_ref, sems, *, steps):
    half = D // 2
    wide = half // 2
    copies = []
    for c in range(4):
        cols = slice((c % 2) * half + (c // 2) * wide, (c % 2) * half + (c // 2 + 1) * wide)
        copies.append(pltpu.make_async_copy(weight_hbm.at[:, cols], weight_ref.at[c], sems.at[c]))
        copies[-1].start()
    for step in range(steps):
        put_shares(probe_ref, slice(step * 128, step * 128 + 128), *probe_step(seeds_ref, hidden_ref, step))
    for c in range(0, 4, 2):
        sides = []
        for side in (c, c + 1):
            copies[side].wait()
            sides.append(jnp.dot(hidden_ref[SKIP:, :], weight_ref[side], preferred_element_type=jnp.float32))
        put_shares(base_ref, slice((c // 2) * wide, (c // 2 + 1) * wide), *sides)


def rest_kernel(seeds_ref, hidden_ref, _, probe_ref, *, first_step):
    put_shares(probe_ref, slice(None), *probe_step(seeds_ref, hidden_ref, pl.program_id(0) + first_step))


def products(seeds, hidden, weight, shares, first_steps=2):
    tokens, units = hidden.shape
    share = (tokens - SKIP) // shares
    half = D // 2
    steps = half // 128
    probe_shape = jax.ShapeDtypeStruct((shares, 2 * share, half), jnp.bfloat16)
    base_shape = jax.ShapeDtypeStruct((shares, 2 * share, half), jnp.float32)
    scalar = pl.BlockSpec(memory_space=pltpu.SMEM)
    whole = pl.BlockSpec((tokens, units), lambda i: (0, 0))
    params = pltpu.CompilerParams(vmem_limit_bytes=44 << 20)

    def cost(count):
        return pl.CostEstimate(flops=units * count * 256 * 2000, bytes_accessed=units * count * 256, transcendentals=0)

    probe, base = pl.pallas_call(
        functools.partial(first_kernel, steps=first_steps),
        grid=(1,),
        in_specs=[scalar, whole, pl.BlockSpec(memory_space=pl.ANY)],
        out_specs=[
            pl.BlockSpec((shares, 2 * share, first_steps * 128), lambda i: (0, 0, 0)),
            pl.BlockSpec((shares, 2 * share, half), lambda i: (0, 0, 0)),
        ],
        out_shape=[probe_shape, base_shape],
        scratch_shapes=[pltpu.VMEM((4, units, half // 2), jnp.bfloat16), pltpu.SemaphoreType.DMA((4,))],
        cost_estimate=cost(first_steps),
        compiler_params=params,
        name="base_and_probe",
    )(seeds, hidden, weight)
    probe = pl.pallas_call(
        functools.partial(rest_kernel, first_step=first_steps),
        grid=(steps - first_steps,),
        in_specs=[scalar, whole, pl.BlockSpec(memory_space=pl.ANY)],
        out_specs=pl.BlockSpec((shares, 2 * share, 128), lambda i: (0, 0, i + first_steps)),
        out_shape=probe_shape,
        input_output_aliases={2: 0},
        cost_estimate=cost(steps - first_steps),
        compiler_params=params,
        name="probe",
    )(seeds, hidden, probe)
    return probe, base


def regenerate_kernel(seeds_ref, out_ref, *, out_rows):
    slabs, depth, width = out_ref.shape
    pairs = seeds_ref.shape[0]
    pop_at, tp_at = places()
    first = (pop_at * lax.axis_size("z") * 2 + tp_at) * out_rows + pl.program_id(0) * (depth // pairs)
    index = seeds_ref[...] * jnp.int32(1540483477) + lax.broadcasted_iota(jnp.int32, (pairs, width), 1)
    for r in range(depth // pairs):
        for c in range(slabs):
            out_ref[c, r * pairs : (r + 1) * pairs, :] = noise_of(index + ((first + r) * D + c * width))


def regenerate(seeds, rows, width=512, rows_each=4):
    pairs = seeds.shape[0]
    return pl.pallas_call(
        functools.partial(regenerate_kernel, out_rows=rows),
        grid=(rows // rows_each,),
        in_specs=[pl.BlockSpec((pairs, 1), lambda i: (0, 0))],
        out_specs=pl.BlockSpec((D // width, rows_each * pairs, width), lambda i: (0, i, 0)),
        out_shape=jax.ShapeDtypeStruct((D // width, rows * pairs, width), jnp.bfloat16),
        cost_estimate=pl.CostEstimate(
            flops=pairs * rows * D * 2000, bytes_accessed=pairs * rows * D * 2, transcendentals=0
        ),
        compiler_params=pltpu.CompilerParams(vmem_limit_bytes=50 << 20),
        name="regenerate",
    )(seeds.reshape(pairs, 1))


def logits_kernel(
    first_ref, rows_hbm, own_hbm, other_hbm, out_ref, rows_ref, heads_ref, held_ref, stats_ref, sems, head_sems
):
    slots, chunk, _ = rows_ref.shape
    chunks = rows_hbm.shape[0] // chunk
    vocab = own_hbm.shape[1]
    lanes = lax.broadcasted_iota(jnp.int32, (1, 128), 1).astype(jnp.float32)

    def fetch(i):
        return pltpu.make_async_copy(
            rows_hbm.at[pl.ds(i * chunk, chunk), :], rows_ref.at[i % slots], sems.at[i % slots]
        )

    third = vocab // 3
    pieces = []
    for hbm, at, cuts in ((own_hbm, 0, (0, 2 * third, vocab)), (other_hbm, vocab, (0, third, vocab))):
        for first, last in zip(cuts[:-1], cuts[1:]):
            to = heads_ref.at[:, at + first : at + last]
            pieces.append(pltpu.make_async_copy(hbm.at[:, first:last], to, head_sems.at[len(pieces)]))

    def multiply(i):
        rows = rows_ref[i % slots, :, :D]
        if i == 0:
            for part, waits in enumerate((pieces[:1], pieces[1:3], pieces[3:])):
                for piece in waits:
                    piece.wait()
                cols = slice(2 * part * third, 2 * (part + 1) * third)
                held_ref[0, :, cols] = jnp.dot(rows, heads_ref[:, cols], preferred_element_type=jnp.float32)
        else:
            held_ref[i % 2] = jnp.dot(rows, heads_ref[...], preferred_element_type=jnp.float32)

    def absorb(i):
        slot = i % 2
        high = held_ref[slot, :, :128]
        for c in range(128, 2 * vocab, 128):
            high = jnp.maximum(high, held_ref[slot, :, c : c + 128])
        high = jnp.broadcast_to(jnp.max(high, axis=1, keepdims=True), (chunk, 128))
        digits = rows_ref[i % slots, :, D : D + EXTRA].astype(jnp.float32)
        label = digits[:, 0:1] * 65536.0 + digits[:, 1:2] * 256.0 + digits[:, 2:3]
        label = [jnp.broadcast_to(label - first_ref[h].astype(jnp.float32), (chunk, 128)) for h in range(2)]
        total = jnp.zeros((chunk, 128), jnp.float32)
        hit = jnp.zeros((chunk, 128), jnp.float32)
        for c in range(0, 2 * vocab, 128):
            slab = held_ref[slot, :, c : c + 128]
            total = total + jnp.exp(slab - high)
            hit = jnp.where(lanes + float(c % vocab) == label[c // vocab], slab, hit)
        total = jnp.sum(total, axis=1, keepdims=True)
        hit = jnp.sum(hit, axis=1, keepdims=True)
        lane = lax.broadcasted_iota(jnp.int32, (chunk, 128), 1)
        stats_ref[i * chunk : (i + 1) * chunk, :] = jnp.where(lane == 0, high + jnp.log(total), hit)

    fetch(0).start()
    for piece in pieces:
        piece.start()
    for i in range(1, min(slots - 1, chunks)):
        fetch(i).start()
    for i in range(chunks):
        fetch(i).wait()
        multiply(i)
        if i:
            absorb(i - 1)
        if i + slots - 1 < chunks:
            fetch(i + slots - 1).start()
    absorb(chunks - 1)
    both = stats_ref[...].T[:2, :]
    for t in range(out_ref.shape[0]):
        out_ref[t] = both


def vocabulary_stats(rows, own_head, other_head, firsts, copies, chunk=512, slots=3):
    count = rows.shape[0]
    vocab = own_head.shape[1]
    return pl.pallas_call(
        logits_kernel,
        in_specs=[
            pl.BlockSpec(memory_space=pltpu.SMEM),
            pl.BlockSpec(memory_space=pl.ANY),
            pl.BlockSpec(memory_space=pl.ANY),
            pl.BlockSpec(memory_space=pl.ANY),
        ],
        out_specs=pl.BlockSpec(memory_space=pltpu.VMEM),
        out_shape=jax.ShapeDtypeStruct((copies, 2, count), jnp.float32),
        scratch_shapes=[
            pltpu.VMEM((slots, chunk, D + EXTRA), jnp.bfloat16),
            pltpu.VMEM((D, 2 * vocab), jnp.bfloat16),
            pltpu.VMEM((2, chunk, 2 * vocab), jnp.float32),
            pltpu.VMEM((count, 128), jnp.float32),
            pltpu.SemaphoreType.DMA((slots,)),
            pltpu.SemaphoreType.DMA((4,)),
        ],
        cost_estimate=pl.CostEstimate(
            flops=2 * count * D * 2 * vocab, bytes_accessed=count * D * 2, transcendentals=0
        ),
        compiler_params=pltpu.CompilerParams(vmem_limit_bytes=54 << 20),
        name="vocabulary_stats",
    )(firsts, rows, own_head, other_head)


def update_kernel(gap_ref, noise_hbm, out_hbm, noise_ref, out_ref, in_sems, out_sems, *, pairs):
    slabs, _, width = noise_ref.shape
    rows = out_ref.shape[1]
    reads = [pltpu.make_async_copy(noise_hbm.at[c], noise_ref.at[c], in_sems.at[c]) for c in range(slabs)]
    writes = [
        pltpu.make_async_copy(out_ref.at[c], out_hbm.at[:, c * width : (c + 1) * width], out_sems.at[c])
        for c in range(slabs)
    ]
    for read in reads:
        read.start()
    gap = gap_ref[...]
    high = gap.astype(jnp.bfloat16).astype(jnp.float32)
    middle = (gap - high).astype(jnp.bfloat16).astype(jnp.float32)
    low = gap - high - middle
    at = (16, 16 * pairs)
    own = lax.broadcasted_iota(jnp.int32, at, 0) * pairs
    lane = lax.broadcasted_iota(jnp.int32, at, 1)
    mine = (lane >= own) & (lane < own + pairs)
    left = jnp.concatenate([jnp.where(mine, jnp.broadcast_to(part, at), 0.0) for part in (high, middle, low)], axis=0)
    left = left.astype(jnp.bfloat16)
    for c in range(slabs):
        reads[c].wait()
        for r in range(0, rows, 16):
            deep = min(16, rows - r)
            parts = jnp.dot(
                left[:, : deep * pairs],
                noise_ref[c, r * pairs : (r + deep) * pairs, :],
                preferred_element_type=jnp.float32,
            )
            total = parts[:16] + parts[16:32] + parts[32:]
            out_ref[c, r : r + deep, :] = total[:deep]
        writes[c].start()
    for write in writes:
        write.wait()


def update(gap, noise, rows):
    slabs, depth, width = noise.shape
    pairs = gap.shape[0]
    return pl.pallas_call(
        functools.partial(update_kernel, pairs=pairs),
        in_specs=[pl.BlockSpec(memory_space=pltpu.VMEM), pl.BlockSpec(memory_space=pl.ANY)],
        out_specs=pl.BlockSpec(memory_space=pl.ANY),
        out_shape=jax.ShapeDtypeStruct((rows, slabs * width), jnp.float32),
        scratch_shapes=[
            pltpu.VMEM((slabs, depth, width), jnp.bfloat16),
            pltpu.VMEM((slabs, rows, width), jnp.float32),
            pltpu.SemaphoreType.DMA((slabs,)),
            pltpu.SemaphoreType.DMA((slabs,)),
        ],
        cost_estimate=pl.CostEstimate(flops=2 * depth * D, bytes_accessed=2 * depth * D, transcendentals=0),
        compiler_params=pltpu.CompilerParams(vmem_limit_bytes=50 << 20),
        name="update",
    )(jnp.tile(gap, 16).reshape(1, 16 * pairs), noise)


def scattered_sum(partial, axes):
    pieces = lax.all_to_all(partial, axes, 0, 0)
    total = jnp.sum(pieces.astype(jnp.float32), axis=0)
    share = total.shape[0] // 2
    return jnp.concatenate([total[:share], total[share:]], axis=1)


def joined(stats, axes):
    everyone = lax.all_to_all(stats, axes, 0, 0)
    level = everyone[:, 0]
    top = jnp.max(level, axis=0)
    level = top + jnp.log(jnp.sum(jnp.exp(level - top[None]), axis=0))
    return jnp.stack([level, jnp.sum(everyone[:, 1], axis=0)])


def local(hidden_units, residual, down_weight, norm_gain, head, labels, answer_start, seeds, signs):
    core = lax.axis_index("core")
    pop_at, tp_at = places()
    tp_count = lax.axis_size("z") * 2
    pop_count = seeds.shape[0]
    chip_pairs = pop_count // 2
    tokens = hidden_units.shape[1]
    scored = tokens - SKIP
    share = scored // tp_count
    vocab = head.shape[1]
    noise_scale = 0.25 * FF ** (-0.5)
    swap = [(0, 1), (1, 0)]

    other_head = lax.ppermute(head, "core", swap)

    probe, base = products(seeds, hidden_units[0], down_weight, tp_count)
    base = scattered_sum(base, TP)
    probe, base = lax.optimization_barrier((probe, base))
    probe = scattered_sum(probe, TP)

    token_at = SKIP + tp_at * share
    pair_signs = lax.dynamic_slice_in_dim(signs, pop_at * 2, 2).astype(jnp.float32)
    own_residual = lax.dynamic_slice_in_dim(residual[0], token_at, share, 0).astype(jnp.float32)
    layer = (own_residual + base)[None] + pair_signs[:, None, None] * noise_scale * probe[None]
    mean_square = jnp.mean(layer * layer, axis=2, keepdims=True)
    normed = (layer * lax.rsqrt(mean_square + 1e-06) * norm_gain).astype(jnp.bfloat16)
    own_labels = lax.dynamic_slice_in_dim(labels[0], token_at, share, 0)
    slots = jnp.arange(EXTRA, dtype=jnp.int32)[None, :]
    digits = (own_labels[:, None] >> jnp.clip(16 - 8 * slots, 0, 16)) & 255
    digits = jnp.where(slots < 3, digits, 0).astype(jnp.bfloat16)
    normed = jnp.concatenate([normed, jnp.broadcast_to(digits[None], (2, share, EXTRA))], axis=2)

    out_rows = FF // (pop_count * tp_count)
    later_seeds, normed = lax.optimization_barrier((seeds, normed))
    rows = lax.all_gather(normed.reshape(2 * share, D + EXTRA), SAME_CORE, axis=0, tiled=True)
    noise = regenerate(later_seeds, out_rows)

    own_vocab = (pop_at * tp_count + tp_at) * vocab
    other_vocab = ((pop_at + 1 - 2 * core) * tp_count + tp_at) * vocab
    firsts, noise = lax.optimization_barrier((jnp.stack([own_vocab, other_vocab]), noise))
    stats = joined(vocabulary_stats(rows, head, other_head, firsts, tp_count), TP)
    stats = joined(jnp.broadcast_to(stats[None], (chip_pairs,) + stats.shape), ("y_lo", "x"))
    log_prob = (stats[1] - stats[0]).reshape(tp_count, chip_pairs, 2, share)
    positions = SKIP + jnp.arange(scored, dtype=jnp.int32).reshape(tp_count, 1, share)
    own_starts = lax.dynamic_index_in_dim(answer_start.reshape(chip_pairs, 2), core, 1, keepdims=False)
    mask = (positions >= own_starts[None, :, None]).astype(jnp.float32)
    own_fitness = jnp.sum(log_prob * mask[:, :, None, :], axis=(0, 3)) / (tokens - own_starts).astype(jnp.float32)[:, None]
    other_fitness = lax.ppermute(own_fitness, "core", swap)
    ordered = jnp.where(
        core == 0,
        jnp.stack([own_fitness, other_fitness], axis=1),
        jnp.stack([other_fitness, own_fitness], axis=1),
    )
    fitness = ordered.reshape(2 * pop_count)
    gap = jnp.sum((fitness * signs.astype(jnp.float32)).reshape(pop_count, 2), axis=1)
    return fitness, update(gap, noise, out_rows)


def solution(mesh):
    fine = Mesh(mesh.devices.reshape(2, 4, 2, 4, 2), ("y_lo", "x", "core", "z", "y_hi"))
    pop = ("y_lo", "x", "core")
    return jax.shard_map(
        local,
        mesh=fine,
        in_specs=(
            P(pop, None, TP),
            P(pop, None, None),
            P(TP, None),
            P(),
            P(None, pop + TP),
            P(pop, None),
            P(),
            P(),
            P(),
        ),
        out_specs=(P(), P(pop + TP, None)),
        check_vma=False,
    )
```
